128 devices in a mesh: pipe: 2 (over core), exp: 8 (over z_hi, y), etp: 8 (over z_lo, x).
Axes of the slice: x: 4, y: 4, z: 4 (z_hi: 2, z_lo: 2; z = z_hi * 2 + z_lo), core: 2. Of those that a mesh axis runs over, the one named last changes fastest.
Arguments:
- inputs: bfloat16 [2, 2048, 3072], P('pipe', 'exp', 'etp'), may hold values from -6 to 6
- attn_gain: bfloat16 [2, 3072], P('pipe'), may hold values from 0.099609375 to 1.8984375
- query_weight: bfloat16 [2, 3072, 3072], P('pipe', None, 'etp'), may hold values from -2 to 2
- key_weight: bfloat16 [2, 3072, 1024], P('pipe', None, 'etp'), may hold values from -2 to 2
- value_weight: bfloat16 [2, 3072, 1024], P('pipe', None, 'etp'), may hold values from -0.109375 to 0.109375
- out_weight: bfloat16 [2, 3072, 3072], P('pipe', 'etp'), may hold values from -0.109375 to 0.109375
- ffn_gain: bfloat16 [2, 3072], P('pipe'), may hold values from 0.099609375 to 1.8984375
- gate_weight: bfloat16 [2, 8, 3072, 8192], P('pipe', 'exp', None, 'etp'), may hold values from -0.109375 to 0.109375
- up_weight: bfloat16 [2, 8, 3072, 8192], P('pipe', 'exp', None, 'etp'), may hold values from -0.109375 to 0.109375
- down_weight: bfloat16 [2, 8, 8192, 3072], P('pipe', 'exp', 'etp'), may hold values from -0.0625 to 0.0625
- expert_ids: int32 [2, 2048, 2], P('pipe', ('exp', 'etp')), may hold values from 0 to 7, all different within a row; in each aligned block of 32 rows (0 to 31, 32 to 63, ..., all dimensions but the last counted through in order) at most 16 rows name the same one
- route_weights: float32 [2, 2048, 2], P('pipe', ('exp', 'etp')), may hold values from 0.2 to 1
Outputs:
- handed: bfloat16 [2, 2048, 3072], P('pipe', ('exp', 'etp'))
The draws below stay inside these ranges and needn't reach their ends.
Inputs may be any that keep to these rules, and one draw needn't show every extreme that they name: `expert_ids`: within the 32 tokens of one device, no expert is named by more than 16 routes, a bound that some block reaches; a token's two experts differ.
All inputs are finite; a program needn't handle non-finite values.
Results may differ from the reference program's by a relative error of at most 0.022.
Values may be sent and summed in bfloat16 or wider, within the bound.
A program may use at most 128 MiB of HBM per device.

```python
import math
import jax
import jax.numpy as jnp
import numpy as np
from jax import lax

D = 3072
HQ = 24
HK = 8
HD = 128
FF = 8192
TOK_DEV = 32
TOKENS = 2048
EXPERTS = 8
CAP = 16
N_PIPE = 2
N_EXP = 8
N_ETP = 8


def draw_query_weight(key, part):
    key = jax.random.fold_in(key, 11)
    base = jnp.clip(jax.random.normal(key, (N_PIPE, D, HQ, HD), jnp.float32), -6.0, 6.0) * D ** (-0.5)
    base = jnp.clip(base, -2.0, 2.0)
    return base.reshape(N_PIPE, D, HQ * HD).astype(jnp.bfloat16)


def draw_key_weight(key, part):
    key = jax.random.fold_in(key, 23)
    base = jnp.clip(jax.random.normal(key, (N_PIPE, D, HK * HD), jnp.float32), -6.0, 6.0) * D ** (-0.5)
    base = jnp.clip(base, -2.0, 2.0)
    return base.astype(jnp.bfloat16)


def block_scale(own_key, extent, split, low, largest):
    factor_of = 1.0
    for dim, blocks in split:
        draws = jax.random.uniform(jax.random.fold_in(jax.random.fold_in(own_key, 6), dim), (blocks,), jnp.float32, low / len(split), largest / len(split))
        factor_of = factor_of * jnp.repeat(jnp.exp(draws), extent[dim] // blocks).reshape((-1,) + (1,) * (len(extent) - 1 - dim))
    return factor_of


def deal_out(stream_key, own, number, rows, amount, top, most, skew):
    sequence = jax.random.permutation(stream_key, amount)
    crowded, usual = portions_of(amount, rows * top, most, skew, True), portions_of(amount, rows * top, most, skew, False)
    places = jnp.arange(amount)

    def named(sizes, offset_by):
        used = int((sizes > 0).sum())
        fixed = max(1, used // 4)
        shifted = fixed + (places - fixed + offset_by * (used - fixed)) % max(1, amount - fixed)
        return jnp.zeros((amount,), jnp.int32).at[sequence[jnp.where(places < fixed, places, shifted)]].set(jnp.asarray(sizes, jnp.int32))

    sizes = jnp.where(number % 4 == 0, named(crowded, number // 4), named(usual, number - number // 4 - 1))
    mixed = jax.random.permutation(jax.random.fold_in(own, 3), amount)
    donor, taker = mixed[0:amount // 2 * 2:2], mixed[1:amount // 2 * 2:2]
    slack = jnp.minimum(sizes[donor] - 1, most - sizes[taker]) // 2
    slack = jnp.where((donor == sequence[0]) | (taker == sequence[0]) | (sizes[taker] == 0), 0, jnp.maximum(slack, 0))
    shifted = jax.random.randint(jax.random.fold_in(own, 4), (amount // 2,), 0, 1 << 20) % (slack + 1)
    sizes = sizes.at[donor].add(-shifted).at[taker].add(shifted)
    members = jnp.searchsorted(jnp.cumsum(sizes), jnp.arange(rows * top), side="right").astype(jnp.int32)
    table = members.reshape(top, rows).T
    table = table[jax.random.permutation(jax.random.fold_in(own, 1), rows)]
    offset_by = jax.random.randint(jax.random.fold_in(own, 2), (rows, 1), 0, top)
    return jnp.take_along_axis(table, (jnp.arange(top)[None, :] + offset_by) % top, axis=1)


def portions_of(number_of, total, limit, slope, full):
    weights = [(1 << 20) // math.isqrt(grade ** slope) + 1 for grade in range(1, number_of + 1)]
    largest = limit if full else min(limit, max(-(-total // number_of), total * weights[0] // sum(weights)))
    least = 1 if total - largest >= number_of - 1 else 0
    holding, spare = [largest] + [least] * (number_of - 1), total - largest - least * (number_of - 1)
    while spare > 0:
        movable = [i for i in range(1, number_of) if holding[i] < largest] or [i for i in range(1, number_of) if holding[i] < limit]
        pool, remaining = sum([weights[i] for i in movable]), spare
        for i in movable:
            more = min(limit - holding[i], max(1, remaining * weights[i] // pool), spare)
            holding[i] = holding[i] + more
            spare = spare - more
    return np.array(holding)


def scatter_about(key, dims, deviation, bound, split=(), kind=jnp.bfloat16):
    result = jax.random.normal(key, dims, jnp.float32) * deviation
    if len(split) > 0:
        result = block_scale(key, dims, split, -0.22, 0.18) * result
    return jnp.clip(result, min=-bound, max=bound).astype(kind)


def setup_inputs(seed: int = 0) -> dict:
    key_list = jax.random.split(jax.random.key(seed), 13)
    inputs = scatter_about(key_list[0], (N_PIPE, TOKENS, D), 1.0, 6.0, ((0, 2), (1, 8), (2, 8)))
    attn_gain = jnp.clip(1.0 + 0.18 * jax.random.normal(key_list[1], (N_PIPE, D), jnp.float32), 0.099609375, 1.8984375).astype(jnp.bfloat16)
    query_weight = draw_query_weight(jax.random.fold_in(key_list[12], 71), 0)
    key_weight = draw_key_weight(jax.random.fold_in(key_list[12], 71), 0)
    value_weight = scatter_about(key_list[4], (N_PIPE, D, HK * HD), D ** -0.5, 0.109375, ((0, 2), (2, 8)))
    out_weight = scatter_about(key_list[5], (N_PIPE, HQ * HD, D), (HQ * HD) ** -0.5, 0.109375, ((0, 2), (1, 8)))
    ffn_gain = jnp.clip(1.0 + 0.18 * jax.random.normal(key_list[6], (N_PIPE, D), jnp.float32), 0.099609375, 1.8984375).astype(jnp.bfloat16)
    gate_weight = scatter_about(key_list[7], (N_PIPE, EXPERTS, D, FF), D ** -0.5, 0.109375, ((0, 2), (1, 8), (3, 8)))
    up_weight = scatter_about(key_list[8], (N_PIPE, EXPERTS, D, FF), D ** -0.5, 0.109375, ((0, 2), (1, 8), (3, 8)))
    down_weight = scatter_about(key_list[9], (N_PIPE, EXPERTS, FF, D), FF ** -0.5, 0.0625, ((0, 2), (1, 8), (2, 8)))
    expert_ids_keys = jax.random.split(jax.random.fold_in(key_list[10], 1), N_PIPE * TOKENS // TOK_DEV)
    expert_ids_turns = jax.random.permutation(jax.random.fold_in(key_list[10], 3), N_PIPE * TOKENS // TOK_DEV)
    expert_ids = jax.vmap(lambda own, number: deal_out(jax.random.fold_in(key_list[10], 2), own, number, TOK_DEV, EXPERTS, 2, CAP, 2))(expert_ids_keys, expert_ids_turns).reshape((N_PIPE, TOKENS, 2))
    route_weights = jnp.clip(0.2 + 0.8 * jax.random.uniform(key_list[11], (N_PIPE, TOKENS, 2), jnp.float32) ** block_scale(key_list[11], (N_PIPE, TOKENS, 2), ((0, 2), (1, 64)), -0.2, 0.2), 0.2, 1.0)
    return dict(inputs=inputs, attn_gain=attn_gain, query_weight=query_weight, key_weight=key_weight, value_weight=value_weight, out_weight=out_weight, ffn_gain=ffn_gain, gate_weight=gate_weight, up_weight=up_weight, down_weight=down_weight, expert_ids=expert_ids, route_weights=route_weights)


epsilon = 1e-05
rope_base = 1000000.0

def rms_scale(values_in, gain):
    floats = values_in.astype(jnp.float32)
    factor = lax.rsqrt(lax.optimization_barrier(jnp.mean(floats * floats, axis=-1, keepdims=True)) + epsilon)
    return (floats * factor * gain.astype(jnp.float32)).astype(jnp.bfloat16)

def rotate(tensor):
    seq_len = tensor.shape[0]
    half_dim = tensor.shape[2] // 2
    freqs = rope_base ** (-jnp.arange(half_dim, dtype=jnp.float32) / half_dim)
    angles = jnp.arange(seq_len, dtype=jnp.float32)[:, None] * freqs[None, :]
    cosine = jnp.cos(angles)[:, None, :]
    sine = jnp.sin(angles)[:, None, :]
    first = tensor[..., :half_dim]
    second = tensor[..., half_dim:]
    return jnp.concatenate([first * cosine - second * sine, second * cosine + first * sine], axis=-1)

def attend(normed, query_w, key_w, value_w, heads_q, heads_k):
    seq_len = normed.shape[0]
    queries = rotate(jnp.dot(normed, query_w, preferred_element_type=jnp.float32).reshape(seq_len, heads_q, HD)).astype(jnp.bfloat16)
    keys_rot = rotate(jnp.dot(normed, key_w, preferred_element_type=jnp.float32).reshape(seq_len, heads_k, HD)).astype(jnp.bfloat16)
    values = jnp.dot(normed, value_w, preferred_element_type=jnp.float32).astype(jnp.bfloat16).reshape(seq_len, heads_k, HD)
    group_ratio = heads_q // heads_k
    grouped = queries.reshape(seq_len, heads_k, group_ratio, HD)
    scores = jnp.einsum('skrd,tkd->krst', grouped.astype(jnp.float32), keys_rot.astype(jnp.float32)) * HD ** (-0.5)
    causal = jnp.arange(seq_len)[:, None] >= jnp.arange(seq_len)[None, :]
    scores = jnp.where(causal, scores, -1e+30)
    peak = lax.optimization_barrier(jnp.max(scores, axis=-1, keepdims=True))
    expo = jnp.exp(scores - peak)
    weights_bf = (expo / lax.optimization_barrier(jnp.sum(expo, axis=-1, keepdims=True))).astype(jnp.bfloat16)
    mixed = jnp.einsum('krst,tkd->skrd', weights_bf.astype(jnp.float32), values.astype(jnp.float32)).astype(jnp.bfloat16)
    return mixed.reshape(seq_len, heads_q * HD)

def reference(inputs, attn_gain, query_weight, key_weight, value_weight, out_weight, ffn_gain, gate_weight, up_weight, down_weight, expert_ids, route_weights):
    experts = N_EXP
    seq_len = TOK_DEV * N_ETP
    all_tokens = seq_len * N_EXP
    blocks = all_tokens // TOK_DEV
    share_width = FF // N_ETP
    results = []
    for section_index in range(N_PIPE):
        pieces = []
        for group_index in range(N_EXP):
            segment = inputs[section_index, group_index * seq_len:(group_index + 1) * seq_len]
            normed = rms_scale(segment, attn_gain[section_index])
            mixed = attend(normed, query_weight[section_index], key_weight[section_index], value_weight[section_index], HQ, HK)
            projected = jnp.dot(mixed, out_weight[section_index], preferred_element_type=jnp.float32)
            pieces.append((segment.astype(jnp.float32) + projected).astype(jnp.bfloat16))
        state = jnp.concatenate(pieces, axis=0)
        ffn_in = rms_scale(state, ffn_gain[section_index])
        block_ids = expert_ids[section_index].reshape(blocks, TOK_DEV * 2)
        onehot = (block_ids[:, :, None] == jnp.arange(experts, dtype=jnp.int32)[None, None, :]).astype(jnp.int32)
        before = jnp.cumsum(onehot, axis=1) - onehot
        slot_of = lax.optimization_barrier(jnp.sum(onehot * before, axis=-1))
        dest = (jnp.arange(blocks, dtype=jnp.int32)[:, None] * (TOK_DEV // 2) + slot_of).reshape(-1).astype(jnp.int32)
        flat_ids = block_ids.reshape(-1).astype(jnp.int32)
        token_of = (jnp.arange(all_tokens * 2, dtype=jnp.int32) // 2).astype(jnp.int32)
        buffer = jnp.zeros((experts, blocks * (TOK_DEV // 2), D), jnp.bfloat16)
        buffer = buffer.at[flat_ids, dest].set(ffn_in[token_of])
        outputs = []
        for expert in range(experts):
            gate = jnp.dot(buffer[expert], gate_weight[section_index, expert], preferred_element_type=jnp.float32)
            upper = jnp.dot(buffer[expert], up_weight[section_index, expert], preferred_element_type=jnp.float32)
            act = (jax.nn.silu(gate) * upper).astype(jnp.bfloat16)
            total = jnp.zeros((act.shape[0], D), jnp.float32)
            for share_index in range(N_ETP):
                lo = share_index * share_width
                share = jnp.dot(act[:, lo:lo + share_width], down_weight[section_index, expert, lo:lo + share_width], preferred_element_type=jnp.float32).astype(jnp.bfloat16)
                total = total + share.astype(jnp.float32)
            outputs.append(total.astype(jnp.bfloat16))
        expert_out = jnp.stack(outputs)
        picked = expert_out[flat_ids, dest].reshape(all_tokens, 2, D).astype(jnp.float32)
        combined = lax.optimization_barrier(jnp.sum(route_weights[section_index][:, :, None].astype(jnp.float32) * picked, axis=1))
        results.append((state.astype(jnp.float32) + combined).astype(jnp.bfloat16))
    return jnp.roll(jnp.stack(results), 1, axis=0)
```

```python
import jax
import jax.numpy as jnp
import numpy as np
from jax import lax
from jax.experimental import pallas as pl
from jax.experimental.pallas import tpu as pltpu
from jax.sharding import PartitionSpec as P

D = 3072
HQ = 24
HK = 8
HD = 128
CAP = 16
SEQ = 256
TOK = 32
COLS = D // 8
QKV = 640
HID = 1024
HALF = D // 2

epsilon = 1e-05
rope_base = 1000000.0

MESH = pl.DeviceIdType.MESH
BF = jnp.bfloat16
F32 = jnp.float32

OWN, Z, L, R, LZ, RZ, O, OZ = range(8)
UNITS = (
    (OWN, 0), (OWN, 1), (Z, 0), (L, 1),
    (R, 1), (L, 0), (R, 0), (Z, 1),
    (LZ, 0), (RZ, 0), (LZ, 1), (RZ, 1),
    (O, 1), (O, 0), (OZ, 0), (OZ, 1),
)
UNIT_AT = {unit: i for i, unit in enumerate(UNITS)}
UNIT_ROWS = 64


def rope_tables():
    half = HD // 2
    angles = np.arange(SEQ)[:, None] * rope_base ** (-np.arange(half) / half)[None, :]
    cosine, sine = np.cos(angles), np.sin(angles)
    return (
        np.concatenate([cosine, cosine], axis=1).astype(np.float32),
        np.concatenate([-sine, sine], axis=1).astype(np.float32),
    )


class Gather:
    def __init__(self, copy, at, own, peers):
        left, right, across = peers

        def plan(place, part, half, device, there):
            source = own(part) if place == OWN else at(place, part, half)
            return lambda: copy(source, at(there, part, half), device)

        steps = {
            "a_z": plan(OWN, 0, None, across, Z),
            "a_l": plan(OWN, 0, None, left, R),
            "a_r": plan(OWN, 0, None, right, L),
            "b_z": plan(OWN, 1, None, across, Z),
            "b_l": plan(OWN, 1, None, left, R),
            "b_r": plan(OWN, 1, None, right, L),
            "za_l": plan(Z, 0, None, left, RZ),
            "za_r": plan(Z, 0, None, right, LZ),
            "lb_r": plan(L, 1, 0, right, O),
            "rb_l": plan(R, 1, 1, left, O),
            "lb_z": plan(L, 1, None, across, LZ),
            "rb_z": plan(R, 1, None, across, RZ),
            "la_r": plan(L, 0, 0, right, O),
            "ra_l": plan(R, 0, 1, left, O),
            "lza_r": plan(LZ, 0, 0, right, OZ),
            "rza_l": plan(RZ, 0, 1, left, OZ),
            "ob_z": plan(O, 1, None, across, OZ),
        }
        self.copies = {name: make() for name, make in steps.items()}

    def start(self, *names):
        for name in names:
            self.copies[name].start()

    def arrive(self, *names):
        for name in names:
            self.copies[name].wait_recv()

    def step(self, number):
        if number == 0:
            self.start("b_r", "b_l", "a_z", "a_r", "a_l", "b_z")
        if number == 1:
            self.arrive("b_r")
            self.start("lb_r", "lb_z")
            self.arrive("b_l")
            self.start("rb_l", "rb_z")
            self.arrive("a_z")
            self.start("za_r", "za_l")
        if number == 2:
            self.arrive("a_r", "a_l")
            self.start("la_r", "ra_l")
            self.arrive("lb_r", "rb_l")
            self.start("ob_z")
            self.arrive("b_z")
        if number == 3:
            self.arrive("za_r", "za_l")
            self.start("lza_r", "rza_l")
            self.arrive("lb_z", "rb_z")
        if number == 4:
            self.arrive("la_r", "ra_l", "lza_r", "rza_l", "ob_z")

    def finish(self):
        for one in self.copies.values():
            one.wait_send()


class Reduce:
    def __init__(self, copy, at, buffers, peers):
        left, right, across = peers
        self.at = at
        self.relay_a, self.full_a, self.across_a, self.across_b, self.relay_b, self.full_b = buffers
        self.copies = {
            "oz_r": copy(at(OZ, 0, 0), self.relay_a.at[2], right),
            "oz_l": copy(at(OZ, 0, 1), self.relay_a.at[3], left),
            "o_r": copy(at(O, 0, 0), self.relay_a.at[0], right),
            "o_l": copy(at(O, 0, 1), self.relay_a.at[1], left),
            "rz_r": copy(at(RZ, 0, None), self.full_a.at[2], right),
            "lz_l": copy(at(LZ, 0, None), self.full_a.at[3], left),
            "r_r": copy(at(R, 0, None), self.full_a.at[0], right),
            "l_l": copy(at(L, 0, None), self.full_a.at[1], left),
            "z_z": copy(at(Z, 0, None), self.across_a, across),
            "b_own": copy(at(Z, 1, None), self.across_b.at[0], across),
            "b_left": copy(at(LZ, 1, None), self.across_b.at[1], across),
            "b_right": copy(at(RZ, 1, None), self.across_b.at[2], across),
            "b_opp": copy(at(OZ, 1, None), self.across_b.at[3], across),
            "bo_r": copy(at(O, 1, 0), self.relay_b.at[0], right),
            "bo_l": copy(at(O, 1, 1), self.relay_b.at[1], left),
            "br_r": copy(at(R, 1, None), self.full_b.at[0], right),
            "bl_l": copy(at(L, 1, None), self.full_b.at[1], left),
        }

    def start(self, *names):
        for name in names:
            self.copies[name].start()

    def arrive(self, *names):
        for name in names:
            self.copies[name].wait_recv()

    def add(self, place, part, half, *terms):
        ref = self.at(place, part, half)
        total = ref[...].astype(F32)
        for term in terms:
            total = total + term[...].astype(F32)
        ref[...] = total.astype(BF)

    def early(self):
        self.start("b_left", "b_right", "b_own")

    def run(self):
        self.start("oz_r", "oz_l", "b_opp", "o_r", "o_l")
        self.arrive("oz_r")
        self.add(RZ, 0, 0, self.relay_a.at[2])
        self.start("rz_r")
        self.arrive("oz_l")
        self.add(LZ, 0, 1, self.relay_a.at[3])
        self.start("lz_l")
        self.arrive("b_opp")
        self.add(O, 1, None, self.across_b.at[3])
        self.start("bo_r", "bo_l")
        self.arrive("o_r")
        self.add(R, 0, 0, self.relay_a.at[0])
        self.start("r_r")
        self.arrive("o_l")
        self.add(L, 0, 1, self.relay_a.at[1])
        self.start("l_l")
        self.arrive("b_right", "b_left")
        self.add(R, 1, None, self.across_b.at[2])
        self.add(L, 1, None, self.across_b.at[1])
        self.arrive("bo_r")
        self.add(R, 1, 0, self.relay_b.at[0])
        self.start("br_r")
        self.arrive("bo_l")
        self.add(L, 1, 1, self.relay_b.at[1])
        self.start("bl_l")
        self.arrive("rz_r", "lz_l")
        self.add(Z, 0, None, self.full_a.at[2], self.full_a.at[3])
        self.start("z_z")
        self.arrive("r_r", "l_l", "b_own", "br_r", "bl_l", "z_z")
        part_a = (
            self.at(OWN, 0, None)[...].astype(F32)
            + self.full_a[0].astype(F32)
            + self.full_a[1].astype(F32)
            + self.across_a[...].astype(F32)
        )
        part_b = (
            self.at(OWN, 1, None)[...].astype(F32)
            + self.across_b[0].astype(F32)
            + self.full_b[0].astype(F32)
            + self.full_b[1].astype(F32)
        )
        return part_a, part_b

    def finish(self):
        for one in self.copies.values():
            one.wait_send()


def layer(
    x_ref, gain1_ref, wq_ref, wk_ref, wv_ref, wo_ref, gain2_ref, wg_ref, wu_ref, wd_ref, ids_ref, weights_ref,
    cos_ref, sin_ref, out_ref,
    wqkv, wo, wg, wu, wd, xs, acc, heads, mixed, proj, state, outgoing, rows, act, part, returned, final,
    p_relay_a, p_full_a, p_across_a, p_across_b, p_relay_b, p_full_b,
    d_relay_a, d_full_a, d_across_a, d_across_b, d_relay_b, d_full_b,
    load_sem, send_sem, recv_sem,
):
    pipe, exp, etp = lax.axis_index("pipe"), lax.axis_index("exp"), lax.axis_index("etp")
    zh, y = exp // 4, exp % 4
    zl, x = etp // 4, etp % 4

    def ring(zl_to, step):
        return zl_to * 4 + (x + step) % 4

    index_of = {
        OWN: etp, Z: ring(1 - zl, 0), L: ring(zl, 3), R: ring(zl, 1),
        LZ: ring(1 - zl, 3), RZ: ring(1 - zl, 1), O: ring(zl, 2), OZ: ring(1 - zl, 2),
    }
    peers = tuple((pipe, exp, index_of[place]) for place in (L, R, Z))

    def exchange(dz, dy):
        zh_to, y_to = (zh + dz) % 2, (y + dy) % 4
        return zh_to * 4 + y_to, y_to, (etp if dz == 0 else index_of[Z])

    hops = [(dz, dy) for dy in (2, 1, 3, 0) for dz in (1, 0) if (dz, dy) != (0, 0)]
    other_core = (1 - pipe, exp, etp)

    barrier = pltpu.get_barrier_semaphore()
    for device in peers:
        pl.semaphore_signal(barrier, inc=1, device_id=device, device_id_type=MESH)
    for dz, dy in hops:
        e_to, _, k_to = exchange(dz, dy)
        pl.semaphore_signal(barrier, inc=1, device_id=(pipe, e_to, k_to), device_id_type=MESH)
    pl.semaphore_signal(barrier, inc=1, device_id=other_core, device_id_type=MESH)

    loads = [
        pltpu.make_async_copy(source, target, load_sem.at[i])
        for i, (source, target) in enumerate(
            (
                (x_ref, xs.at[0]),
                (wq_ref, wqkv.at[:, pl.ds(0, 384)]),
                (wk_ref, wqkv.at[:, pl.ds(384, 128)]),
                (wv_ref, wqkv.at[:, pl.ds(512, 128)]),
                (wo_ref, wo),
                (wg_ref, wg),
                (wu_ref, wu),
                (wd_ref, wd),
            )
        )
    ]
    for one in loads:
        one.start()
    pl.semaphore_wait(barrier, 4 + len(hops))

    used = [0]

    def copy(source, target, device):
        i = used[0]
        used[0] = i + 1
        return pltpu.make_async_remote_copy(
            src_ref=source, dst_ref=target, send_sem=send_sem.at[i], recv_sem=recv_sem.at[i],
            device_id=device, device_id_type=MESH,
        )

    def xs_at(place, part_no, half):
        first, count = part_no * 128, 128
        if half is not None:
            first, count = first + half * 64, 64
        return xs.at[place, pl.ds(first, count)]

    features = Gather(copy, xs_at, lambda part_no: x_ref.at[pl.ds(part_no * 128, 128)], peers)
    squares = []

    def project(place):
        offset = pl.multiple_of(index_of[place] * COLS, 128)
        block = xs[place].astype(F32)
        squares.append(jnp.sum(block * block, axis=1, keepdims=True))
        scaled = (block * gain1_ref[:, pl.ds(offset, COLS)].astype(F32)).astype(BF)
        term = jnp.dot(scaled, wqkv[pl.ds(offset, COLS), :], preferred_element_type=F32)
        acc[...] = term if place == OWN else acc[...] + term
        own_rows = pl.ds(pl.multiple_of(etp * TOK, TOK), TOK)
        state[:, pl.ds(offset, COLS)] = xs[place, own_rows, :].astype(F32)

    features.step(0)
    for one in loads[:4]:
        one.wait()
    project(OWN)
    features.step(1)
    features.step(2)
    for place in (Z, L, R):
        project(place)
    features.step(3)
    for place in (LZ, RZ):
        project(place)
    features.step(4)
    for place in (O, OZ):
        project(place)

    factor = lax.rsqrt(sum(squares) * (1.0 / D) + epsilon)
    for i in range(5):
        block = acc[:, i * HD : (i + 1) * HD] * factor
        if i < 4:
            block = block * cos_ref[...] + pltpu.roll(block, HD // 2, 1) * sin_ref[...]
        heads[:, i * HD : (i + 1) * HD] = block.astype(BF)
    causal = lax.broadcasted_iota(jnp.int32, (SEQ, SEQ), 0) >= lax.broadcasted_iota(jnp.int32, (SEQ, SEQ), 1)
    keys, values = heads[:, 384:512], heads[:, 512:640]
    for i in range(3):
        scores = lax.dot_general(
            heads[:, i * HD : (i + 1) * HD], keys, (((1,), (1,)), ((), ())), preferred_element_type=F32
        ) * HD ** (-0.5)
        scores = jnp.where(causal, scores, -1e30)
        expo = jnp.exp(scores - jnp.max(scores, axis=1, keepdims=True))
        probs = (expo / jnp.sum(expo, axis=1, keepdims=True)).astype(BF)
        mixed[:, i * HD : (i + 1) * HD] = jnp.dot(probs, values, preferred_element_type=F32).astype(BF)
    loads[4].wait()

    def out_columns(n, carry):
        columns = pl.ds(pl.multiple_of(n * 512, 512), 512)
        proj[:, columns] = jnp.dot(mixed[...], wo[:, columns], preferred_element_type=F32).astype(BF)
        return carry

    lax.fori_loop(0, D // 512, out_columns, 0)

    def proj_at(place, part_no, half):
        first = pl.multiple_of(index_of[place] * TOK + part_no * 16, 16)
        columns = pl.ds(0, D) if half is None else pl.ds(half * HALF, HALF)
        return proj.at[pl.ds(first, 16), columns]

    attention = Reduce(
        copy, proj_at, (p_relay_a, p_full_a, p_across_a, p_across_b, p_relay_b, p_full_b), peers
    )
    attention.early()

    slot_row = lax.broadcasted_iota(jnp.int32, (8 * CAP, TOK), 0)
    first_route = (ids_ref[0:1, :] == slot_row // CAP).astype(F32)
    second_route = (ids_ref[1:2, :] == slot_row // CAP).astype(F32)
    routed = first_route + second_route
    earlier = (
        lax.broadcasted_iota(jnp.int32, (TOK, TOK), 0) < lax.broadcasted_iota(jnp.int32, (TOK, TOK), 1)
    ).astype(BF)
    before = jnp.dot(routed.astype(BF), earlier, preferred_element_type=F32)
    here = (before == (slot_row % CAP).astype(F32)).astype(F32)
    table = routed * here
    combine = (first_route * weights_ref[0:1, :] + second_route * weights_ref[1:2, :]) * here

    sum_a, sum_b = attention.run()
    state[0:16, :] = (state[0:16, :] + sum_a).astype(BF).astype(F32)
    state[16:32, :] = (state[16:32, :] + sum_b).astype(BF).astype(F32)
    tokens = state[...]
    factor2 = lax.rsqrt(jnp.mean(tokens * tokens, axis=1, keepdims=True) + epsilon)
    ffn_in = (tokens * factor2 * gain2_ref[...].astype(F32)).astype(BF)
    outgoing[...] = jnp.dot(table.astype(BF), ffn_in, preferred_element_type=F32).astype(BF)

    sends = []
    for dz, dy in hops:
        e_to, _, k_to = exchange(dz, dy)
        sends.append(
            copy(
                outgoing.at[pl.ds(pl.multiple_of(e_to * CAP, CAP), CAP)],
                rows.at[pl.ds(pl.multiple_of(dz * UNIT_ROWS + y * CAP, CAP), CAP)],
                (pipe, e_to, k_to),
            )
        )
        sends[-1].start()
    rows[pl.ds(pl.multiple_of(y * CAP, CAP), CAP), :] = outgoing[pl.ds(pl.multiple_of(exp * CAP, CAP), CAP), :]
    for one in sends:
        one.wait_recv()
    for one in loads[5:]:
        one.wait()

    def rows_at(ref):
        def at(place, part_no, half):
            first, count = UNIT_AT[place, part_no] * UNIT_ROWS, UNIT_ROWS
            if half is not None:
                first, count = first + half * (UNIT_ROWS // 2), UNIT_ROWS // 2
            return ref.at[pl.ds(first, count)]

        return at

    def part_at(place, part_no, half):
        columns = pl.ds(0, D) if half is None else pl.ds(half * HALF, HALF)
        return part.at[pl.ds(UNIT_AT[place, part_no] * UNIT_ROWS, UNIT_ROWS), columns]

    dispatch = Gather(copy, rows_at(rows), lambda part_no: rows_at(rows)(OWN, part_no, None), peers)
    shares = Reduce(
        copy, part_at, (d_relay_a, d_full_a, d_across_a, d_across_b, d_relay_b, d_full_b), peers
    )
    dispatch.step(0)

    def expert(group, carry):
        for number in range(4):

            @pl.when(group == number)
            def _(number=number):
                dispatch.step(number + 1)
                if number == 3:
                    shares.early()

        here_rows = pl.ds(pl.multiple_of(group * 256, 256), 256)

        def hidden(n, inner):
            columns = pl.ds(pl.multiple_of(n * 512, 512), 512)
            block = rows[here_rows, :]
            gate = jnp.dot(block, wg[:, columns], preferred_element_type=F32)
            upper = jnp.dot(block, wu[:, columns], preferred_element_type=F32)
            act[:, columns] = (gate / (1.0 + jnp.exp(-gate)) * upper).astype(BF)
            return inner

        lax.fori_loop(0, HID // 512, hidden, 0)

        def down(n, inner):
            columns = pl.ds(pl.multiple_of(n * 512, 512), 512)
            part[here_rows, columns] = jnp.dot(act[...], wd[:, columns], preferred_element_type=F32).astype(BF)
            return inner

        lax.fori_loop(0, D // 512, down, 0)
        return carry

    lax.fori_loop(0, 4, expert, 0)

    sum_a, sum_b = shares.run()
    final[0:UNIT_ROWS, :] = sum_a.astype(BF)
    final[UNIT_ROWS:, :] = sum_b.astype(BF)

    own_slots = pl.ds(pl.multiple_of(exp * CAP, CAP), CAP)
    backs = []
    for dz, dy in hops:
        e_to, y_to, k_to = exchange(dz, dy)
        backs.append(
            copy(
                final.at[pl.ds(pl.multiple_of(dz * UNIT_ROWS + y_to * CAP, CAP), CAP)],
                returned.at[own_slots],
                (pipe, e_to, k_to),
            )
        )
        backs[-1].start()
    returned[own_slots, :] = final[pl.ds(pl.multiple_of(y * CAP, CAP), CAP), :]
    combine_high = combine.astype(BF)
    combine_low = (combine - combine_high.astype(F32)).astype(BF)
    for one in backs:
        one.wait_recv()
    over_slots = (((0,), (0,)), ((), ()))
    moe = lax.dot_general(combine_high, returned[...], over_slots, preferred_element_type=F32)
    moe = moe + lax.dot_general(combine_low, returned[...], over_slots, preferred_element_type=F32)
    state[...] = state[...] + moe
    outgoing_final = final.at[pl.ds(0, TOK)]
    for one in backs:
        one.wait_send()
    outgoing_final[...] = state[...].astype(BF)
    handed = copy(outgoing_final, out_ref, other_core)
    handed.start()
    for one in (features, attention, dispatch, shares):
        one.finish()
    for one in sends:
        one.wait_send()
    handed.wait()


def buffers(part_rows):
    return [
        pltpu.VMEM((4, part_rows, HALF), BF),
        pltpu.VMEM((4, part_rows, D), BF),
        pltpu.VMEM((part_rows, D), BF),
        pltpu.VMEM((4, part_rows, D), BF),
        pltpu.VMEM((2, part_rows, HALF), BF),
        pltpu.VMEM((2, part_rows, D), BF),
    ]


def on_device(
    inputs,
    attn_gain,
    query_weight,
    key_weight,
    value_weight,
    out_weight,
    ffn_gain,
    gate_weight,
    up_weight,
    down_weight,
    expert_ids,
    route_weights,
):
    cosine, sine = rope_tables()
    anywhere = pl.BlockSpec(memory_space=pl.ANY)
    vmem = pl.BlockSpec(memory_space=pltpu.VMEM)
    handed = pl.pallas_call(
        layer,
        out_shape=jax.ShapeDtypeStruct((TOK, D), BF),
        in_specs=[anywhere, vmem] + [anywhere] * 4 + [vmem] + [anywhere] * 3 + [vmem] * 4,
        out_specs=anywhere,
        scratch_shapes=[
            pltpu.VMEM((D, QKV), BF),
            pltpu.VMEM((384, D), BF),
            pltpu.VMEM((D, HID), BF),
            pltpu.VMEM((D, HID), BF),
            pltpu.VMEM((HID, D), BF),
            pltpu.VMEM((8, SEQ, COLS), BF),
            pltpu.VMEM((SEQ, QKV), F32),
            pltpu.VMEM((SEQ, QKV), BF),
            pltpu.VMEM((SEQ, 384), BF),
            pltpu.VMEM((SEQ, D), BF),
            pltpu.VMEM((TOK, D), F32),
            pltpu.VMEM((8 * CAP, D), BF),
            pltpu.VMEM((16 * UNIT_ROWS, D), BF),
            pltpu.VMEM((256, HID), BF),
            pltpu.VMEM((16 * UNIT_ROWS, D), BF),
            pltpu.VMEM((8 * CAP, D), BF),
            pltpu.VMEM((2 * UNIT_ROWS, D), BF),
            *buffers(16),
            *buffers(UNIT_ROWS),
            pltpu.SemaphoreType.DMA((8,)),
            pltpu.SemaphoreType.DMA((96,)),
            pltpu.SemaphoreType.DMA((96,)),
        ],
        compiler_params=pltpu.CompilerParams(
            collective_id=0, has_side_effects=True, vmem_limit_bytes=60 * 2**20
        ),
        cost_estimate=pl.CostEstimate(flops=22_000_000_000, bytes_accessed=26_000_000, transcendentals=0),
        name="layer",
    )(
        inputs[0],
        attn_gain,
        query_weight[0],
        key_weight[0],
        value_weight[0],
        out_weight[0],
        ffn_gain,
        gate_weight[0, 0],
        up_weight[0, 0],
        down_weight[0, 0],
        expert_ids[0].T,
        route_weights[0].T,
        jnp.asarray(cosine),
        jnp.asarray(sine),
    )
    return handed[None]


def solution(mesh):
    in_specs = (
        P("pipe", "exp", "etp"),
        P("pipe", None),
        P("pipe", None, "etp"),
        P("pipe", None, "etp"),
        P("pipe", None, "etp"),
        P("pipe", "etp", None),
        P("pipe", None),
        P("pipe", "exp", None, "etp"),
        P("pipe", "exp", None, "etp"),
        P("pipe", "exp", "etp", None),
        P("pipe", ("exp", "etp"), None),
        P("pipe", ("exp", "etp"), None),
    )
    out_specs = P("pipe", ("exp", "etp"), None)
    return jax.shard_map(
        on_device, mesh=mesh, in_specs=in_specs, out_specs=out_specs, check_vma=False
    )
```

```python
import jax
import jax.numpy as jnp
import numpy as np
from jax import lax
from jax.experimental import pallas as pl
from jax.experimental.pallas import tpu as pltpu
from jax.sharding import PartitionSpec as P

D = 3072
HQ = 24
HK = 8
HD = 128
CAP = 16
SEQ = 256
TOK = 32
COLS = D // 8
QKV = 640
HID = 1024

epsilon = 1e-05
rope_base = 1000000.0

MESH = pl.DeviceIdType.MESH
BF = jnp.bfloat16
F32 = jnp.float32

OWN, Z, L, R, LZ, RZ, O, OZ = range(8)
SLOTS = 8 * CAP
PART_SLOTS = SLOTS // 2
SPLIT = 2048
SPLIT_BACK = 2048
META = 16
X_ROWS = SEQ + META


def rope_tables():
    half = HD // 2
    angles = np.arange(SEQ)[:, None] * rope_base ** (-np.arange(half) / half)[None, :]
    cosine, sine = np.cos(angles), np.sin(angles)
    return (
        np.concatenate([cosine, cosine], axis=1).astype(np.float32),
        np.concatenate([-sine, sine], axis=1).astype(np.float32),
    )


class Gather:
    def __init__(self, copy, at, peers):
        left, right, across = peers

        def plan(place, part, half, device, there):
            return lambda: copy(at(place, part, half), at(there, part, half), device)

        steps = {
            "a_z": plan(OWN, 0, None, across, Z),
            "a_l": plan(OWN, 0, None, left, R),
            "a_r": plan(OWN, 0, None, right, L),
            "b_z": plan(OWN, 1, None, across, Z),
            "b_l": plan(OWN, 1, None, left, R),
            "b_r": plan(OWN, 1, None, right, L),
            "za_l": plan(Z, 0, None, left, RZ),
            "za_r": plan(Z, 0, None, right, LZ),
            "lb_r": plan(L, 1, 0, right, O),
            "rb_l": plan(R, 1, 1, left, O),
            "lb_z": plan(L, 1, None, across, LZ),
            "rb_z": plan(R, 1, None, across, RZ),
            "la_r": plan(L, 0, 0, right, O),
            "ra_l": plan(R, 0, 1, left, O),
            "lza_r": plan(LZ, 0, 0, right, OZ),
            "rza_l": plan(RZ, 0, 1, left, OZ),
            "ob_z": plan(O, 1, None, across, OZ),
        }
        self.copies = {name: make() for name, make in steps.items()}

    def start(self, *names):
        for name in names:
            self.copies[name].start()

    def arrive(self, *names):
        for name in names:
            self.copies[name].wait_recv()

    def step(self, number):
        if number == 0:
            self.start("b_r", "b_l", "a_z", "a_r", "a_l", "b_z")
        if number == 1:
            self.arrive("b_r")
            self.start("lb_r", "lb_z")
            self.arrive("b_l")
            self.start("rb_l", "rb_z")
            self.arrive("a_z")
            self.start("za_r", "za_l")
            self.arrive("b_z")
        if number == 2:
            self.arrive("a_r", "a_l")
            self.start("la_r", "ra_l")
            self.arrive("lb_r", "rb_l")
            self.start("ob_z")
        if number == 3:
            self.arrive("za_r", "za_l")
            self.start("lza_r", "rza_l")
            self.arrive("lb_z", "rb_z")
        if number == 4:
            self.arrive("la_r", "ra_l", "lza_r", "rza_l", "ob_z")

    def finish(self):
        for one in self.copies.values():
            one.wait_send()


class Reduce:
    def __init__(self, copy, at, buffers, peers):
        left, right, across = peers
        self.at = at
        self.relay_a, self.full_a, self.across_a, self.across_b, self.relay_b, self.full_b = buffers
        self.copies = {
            "oz_r": copy(at(OZ, 0, 0), self.relay_a.at[2], right),
            "oz_l": copy(at(OZ, 0, 1), self.relay_a.at[3], left),
            "o_r": copy(at(O, 0, 0), self.relay_a.at[0], right),
            "o_l": copy(at(O, 0, 1), self.relay_a.at[1], left),
            "rz_r": copy(at(RZ, 0, None), self.full_a.at[2], right),
            "lz_l": copy(at(LZ, 0, None), self.full_a.at[3], left),
            "r_r": copy(at(R, 0, None), self.full_a.at[0], right),
            "l_l": copy(at(L, 0, None), self.full_a.at[1], left),
            "z_z": copy(at(Z, 0, None), self.across_a, across),
            "b_own": copy(at(Z, 1, None), self.across_b.at[0], across),
            "b_left": copy(at(LZ, 1, None), self.across_b.at[1], across),
            "b_right": copy(at(RZ, 1, None), self.across_b.at[2], across),
            "b_opp": copy(at(OZ, 1, None), self.across_b.at[3], across),
            "bo_r": copy(at(O, 1, 0), self.relay_b.at[0], right),
            "bo_l": copy(at(O, 1, 1), self.relay_b.at[1], left),
            "br_r": copy(at(R, 1, None), self.full_b.at[0], right),
            "bl_l": copy(at(L, 1, None), self.full_b.at[1], left),
        }

    def start(self, *names):
        for name in names:
            self.copies[name].start()

    def arrive(self, *names):
        for name in names:
            self.copies[name].wait_recv()

    def add(self, place, part, half, *terms):
        ref = self.at(place, part, half)
        total = ref[...].astype(F32)
        for term in terms:
            total = total + term[...].astype(F32)
        ref[...] = total.astype(BF)

    def early(self):
        self.start("b_left", "b_right", "b_own")

    def run(self):
        self.start("oz_r", "oz_l", "b_opp", "o_r", "o_l")
        yield
        self.arrive("oz_r")
        self.add(RZ, 0, 0, self.relay_a.at[2])
        self.start("rz_r")
        self.arrive("oz_l")
        self.add(LZ, 0, 1, self.relay_a.at[3])
        self.start("lz_l")
        yield
        self.arrive("b_opp")
        self.add(O, 1, None, self.across_b.at[3])
        self.start("bo_r", "bo_l")
        yield
        self.arrive("o_r")
        self.add(R, 0, 0, self.relay_a.at[0])
        self.start("r_r")
        self.arrive("o_l")
        self.add(L, 0, 1, self.relay_a.at[1])
        self.start("l_l")
        yield
        self.arrive("b_right", "b_left")
        self.add(R, 1, None, self.across_b.at[2])
        self.add(L, 1, None, self.across_b.at[1])
        self.arrive("bo_r")
        self.add(R, 1, 0, self.relay_b.at[0])
        self.start("br_r")
        self.arrive("bo_l")
        self.add(L, 1, 1, self.relay_b.at[1])
        self.start("bl_l")
        yield
        self.arrive("rz_r", "lz_l")
        self.add(Z, 0, None, self.full_a.at[2], self.full_a.at[3])
        self.start("z_z")
        yield
        self.arrive("r_r", "l_l", "b_own", "br_r", "bl_l")
        part_b = (
            self.at(OWN, 1, None)[...].astype(F32)
            + self.across_b[0].astype(F32)
            + self.full_b[0].astype(F32)
            + self.full_b[1].astype(F32)
        )
        part_a = (
            self.at(OWN, 0, None)[...].astype(F32)
            + self.full_a[0].astype(F32)
            + self.full_a[1].astype(F32)
        )
        self.arrive("z_z")
        self.sums = part_a + self.across_a[...].astype(F32), part_b

    def finish(self):
        for one in self.copies.values():
            one.wait_send()


def placed(first_ids, second_ids):
    slot_row = lax.broadcasted_iota(jnp.int32, (SLOTS, TOK), 0)
    expert = (slot_row // CAP).astype(F32)
    first_route = (first_ids == expert).astype(F32)
    second_route = (second_ids == expert).astype(F32)
    earlier = (
        lax.broadcasted_iota(jnp.int32, (TOK, TOK), 0) < lax.broadcasted_iota(jnp.int32, (TOK, TOK), 1)
    ).astype(BF)
    before = jnp.dot((first_route + second_route).astype(BF), earlier, preferred_element_type=F32)
    here = (before == (slot_row % CAP).astype(F32)).astype(F32)
    return first_route * here, second_route * here


def split_in_three(values):
    high = values.astype(BF).astype(F32)
    middle = (values - high).astype(BF).astype(F32)
    return high, middle, values - high - middle


def layer(
    x_ref, gain1_ref, wq_ref, wk_ref, wv_ref, wo_ref, gain2_ref, wg_ref, wu_ref, wd_ref, ids_ref, weights_ref,
    cos_ref, sin_ref, out_ref,
    wqkv, wo, wg, wu, wd, xs, acc, heads, mixed, proj, state, tables, combine, outgoing, tokens, wide_out, rows, act,
    part, final, returned, wide_back, moe, handed,
    p_relay_a, p_full_a, p_across_a, p_across_b, p_relay_b, p_full_b,
    d_relay_a, d_full_a, d_across_a, d_across_b, d_relay_b, d_full_b,
    m_relay_a, m_full_a, m_across_a, m_across_b, m_relay_b, m_full_b,
    load_sem, send_sem, recv_sem,
):
    pipe, exp, etp = lax.axis_index("pipe"), lax.axis_index("exp"), lax.axis_index("etp")
    zh, y = exp // 4, exp % 4
    zl, x = etp // 4, etp % 4

    def ring(zl_to, step):
        return zl_to * 4 + (x + step) % 4

    index_of = {
        OWN: etp, Z: ring(1 - zl, 0), L: ring(zl, 3), R: ring(zl, 1),
        LZ: ring(1 - zl, 3), RZ: ring(1 - zl, 1), O: ring(zl, 2), OZ: ring(1 - zl, 2),
    }
    peers = tuple((pipe, exp, index_of[place]) for place in (L, R, Z))

    def exchange(dz, dy):
        zh_to, y_to = (zh + dz) % 2, (y + dy) % 4
        return zh_to * 4 + y_to, y_to, (etp if dz == 0 else index_of[Z])

    hops = [(dz, dy) for dy in (2, 1, 3, 0) for dz in (1, 0) if (dz, dy) != (0, 0)]
    other_core = (1 - pipe, exp, etp)

    barrier = pltpu.get_barrier_semaphore()
    for device in peers:
        pl.semaphore_signal(barrier, inc=1, device_id=device, device_id_type=MESH)
    for dz, dy in hops:
        e_to, _, k_to = exchange(dz, dy)
        pl.semaphore_signal(barrier, inc=1, device_id=(pipe, e_to, k_to), device_id_type=MESH)
    pl.semaphore_signal(barrier, inc=1, device_id=other_core, device_id_type=MESH)

    loads = [
        pltpu.make_async_copy(source, target, load_sem.at[i])
        for i, (source, target) in enumerate(
            (
                (x_ref, xs.at[0, pl.ds(0, SEQ)]),
                (wq_ref, wqkv.at[:, pl.ds(0, 384)]),
                (wk_ref, wqkv.at[:, pl.ds(384, 128)]),
                (wv_ref, wqkv.at[:, pl.ds(512, 128)]),
                (wo_ref, wo),
                (wg_ref, wg),
                (wu_ref, wu),
                (wd_ref, wd),
            )
        )
    ]
    for one in loads:
        one.start()

    xs[0, SEQ:X_ROWS, :] = jnp.zeros((META, COLS), BF)
    meta_row = lax.broadcasted_iota(jnp.int32, (META, TOK), 0)
    meta_rows = [ids_ref[0:1, :].astype(F32), ids_ref[1:2, :].astype(F32)]
    meta_rows += [*split_in_three(weights_ref[0:1, :]), *split_in_three(weights_ref[1:2, :])]
    meta = jnp.zeros((META, TOK), F32)
    for i, row in enumerate(meta_rows):
        meta = jnp.where(meta_row == i, row, meta)
    xs[0, SEQ:X_ROWS, 0:TOK] = meta.astype(BF)
    loads[0].wait()
    pl.semaphore_wait(barrier, 4 + len(hops))

    used = [0]

    def copy(source, target, device):
        i = used[0]
        used[0] = i + 1
        return pltpu.make_async_remote_copy(
            src_ref=source, dst_ref=target, send_sem=send_sem.at[i], recv_sem=recv_sem.at[i],
            device_id=device, device_id_type=MESH,
        )

    x_parts = {
        (0, None): (0, 144), (0, 0): (0, 80), (0, 1): (80, 64),
        (1, None): (144, 128), (1, 0): (144, 64), (1, 1): (208, 64),
    }

    def xs_at(place, part_no, half):
        return xs.at[place, pl.ds(*x_parts[part_no, half])]

    features = Gather(copy, xs_at, peers)
    squares = []

    def project(place):
        offset = pl.multiple_of(index_of[place] * COLS, 128)
        block = xs[place, 0:SEQ, :].astype(F32)
        squares.append(jnp.sum(block * block, axis=1, keepdims=True))
        scaled = (block * gain1_ref[:, pl.ds(offset, COLS)].astype(F32)).astype(BF)
        term = jnp.dot(scaled, wqkv[pl.ds(offset, COLS), :], preferred_element_type=F32)
        acc[...] = term if place == OWN else acc[...] + term
        own_rows = pl.ds(pl.multiple_of(etp * TOK, TOK), TOK)
        state[:, pl.ds(offset, COLS)] = xs[place, own_rows, :].astype(F32)

    features.step(0)
    for one in loads[1:4]:
        one.wait()
    project(OWN)
    features.step(1)
    features.step(2)
    for place in (Z, L, R):
        project(place)
    features.step(3)
    for place in (LZ, RZ):
        project(place)
    features.step(4)
    for place in (O, OZ):
        project(place)

    factor = lax.rsqrt(sum(squares) * (1.0 / D) + epsilon)
    for i in range(5):
        block = acc[:, i * HD : (i + 1) * HD] * factor
        if i < 4:
            block = block * cos_ref[...] + pltpu.roll(block, HD // 2, 1) * sin_ref[...]
        heads[:, i * HD : (i + 1) * HD] = block.astype(BF)
    causal = lax.broadcasted_iota(jnp.int32, (SEQ, SEQ), 0) >= lax.broadcasted_iota(jnp.int32, (SEQ, SEQ), 1)
    keys, values = heads[:, 384:512], heads[:, 512:640]
    for i in range(3):
        scores = lax.dot_general(
            heads[:, i * HD : (i + 1) * HD], keys, (((1,), (1,)), ((), ())), preferred_element_type=F32
        ) * HD ** (-0.5)
        scores = jnp.where(causal, scores, -1e30)
        expo = jnp.exp(scores - jnp.max(scores, axis=1, keepdims=True))
        probs = (expo / jnp.sum(expo, axis=1, keepdims=True)).astype(BF)
        mixed[:, i * HD : (i + 1) * HD] = jnp.dot(probs, values, preferred_element_type=F32).astype(BF)
    loads[4].wait()

    def out_columns(n, carry):
        columns = pl.ds(pl.multiple_of(n * 512, 512), 512)
        proj[:, columns] = jnp.dot(mixed[...], wo[:, columns], preferred_element_type=F32).astype(BF)
        return carry

    lax.fori_loop(0, D // 512, out_columns, 0)

    def proj_at(place, part_no, half):
        first = pl.multiple_of(index_of[place] * TOK + part_no * 16, 16)
        columns = pl.ds(0, D) if half is None else pl.ds(half * (D // 2), D // 2)
        return proj.at[pl.ds(first, 16), columns]

    attention = Reduce(
        copy, proj_at, (p_relay_a, p_full_a, p_across_a, p_across_b, p_relay_b, p_full_b), peers
    )
    attention.early()
    running = attention.run()
    next(running)

    for place in range(8):
        sent = xs[place, SEQ:X_ROWS, 0:TOK].astype(F32)
        first_route, second_route = placed(sent[0:1], sent[1:2])
        tables[place] = (first_route + second_route).astype(BF)
        weight = first_route * (sent[2:3] + sent[3:4] + sent[4:5])
        weight = weight + second_route * (sent[5:6] + sent[6:7] + sent[7:8])
        high = weight.astype(BF)
        combine[0, place] = high
        combine[1, place] = (weight - high.astype(F32)).astype(BF)

    def combined(place, outputs):
        over_slots = (((0,), (0,)), ((), ()))
        total = lax.dot_general(combine[0, place], outputs, over_slots, preferred_element_type=F32)
        return total + lax.dot_general(combine[1, place], outputs, over_slots, preferred_element_type=F32)

    for _ in running:
        pass
    sum_a, sum_b = attention.sums
    state[0:16, :] = (state[0:16, :] + sum_a).astype(BF).astype(F32)
    state[16:32, :] = (state[16:32, :] + sum_b).astype(BF).astype(F32)
    state_now = state[...]
    factor2 = lax.rsqrt(jnp.mean(state_now * state_now, axis=1, keepdims=True) + epsilon)
    ffn_in = (state_now * factor2 * gain2_ref[...].astype(F32)).astype(BF)

    tokens[OWN] = ffn_in[:, SPLIT:]

    def halves_at(ref, first_rows, rows_each, first_columns, width):
        def at(place, part_no, half):
            columns = pl.ds(first_columns, width)
            if half is not None:
                columns = pl.ds(first_columns + half * (width // 2), width // 2)
            return ref.at[place, pl.ds(first_rows + part_no * rows_each, rows_each), columns]

        return at

    spread = Gather(copy, halves_at(tokens, 0, 16, 0, D - SPLIT), peers)
    spread.step(0)

    outgoing[...] = jnp.dot(tables[OWN], ffn_in[:, :SPLIT], preferred_element_type=F32).astype(BF)
    sends = []
    for dz, dy in hops:
        e_to, _, k_to = exchange(dz, dy)
        sends.append(
            copy(
                outgoing.at[pl.ds(pl.multiple_of(e_to * CAP, CAP), CAP)],
                rows.at[OWN, pl.ds(pl.multiple_of(dz * PART_SLOTS + y * CAP, CAP), CAP), pl.ds(0, SPLIT)],
                (pipe, e_to, k_to),
            )
        )
        sends[-1].start()
    own_slots = pl.ds(pl.multiple_of(exp * CAP, CAP), CAP)
    own_block = pl.ds(pl.multiple_of(y * CAP, CAP), CAP)
    rows[OWN, own_block, 0:SPLIT] = outgoing[own_slots, :]

    wide_sends = []

    def widen(group):
        for place in (2 * group, 2 * group + 1):
            block = jnp.dot(tables[place], tokens[place], preferred_element_type=F32).astype(BF)
            wide_out[:, place] = block.reshape(8, CAP, D - SPLIT)
        copies = []
        for dz, dy in hops:
            e_to, _, k_to = exchange(dz, dy)
            copies.append(
                copy(
                    wide_out.at[e_to, pl.ds(2 * group, 2)],
                    rows.at[
                        pl.ds(2 * group, 2),
                        pl.ds(pl.multiple_of(dz * PART_SLOTS + y * CAP, CAP), CAP),
                        pl.ds(SPLIT, D - SPLIT),
                    ],
                    (pipe, e_to, k_to),
                )
            )
            copies[-1].start()
        for place in (2 * group, 2 * group + 1):
            rows[place, own_block, SPLIT:] = wide_out[exp, place]
        wide_sends.append(copies)

    spread.step(1)
    widen(0)
    spread.step(2)
    widen(1)
    spread.step(3)
    widen(2)
    spread.step(4)
    widen(3)

    dispatch = Gather(copy, lambda place, part_no, half: rows.at[
        place,
        pl.ds(part_no * PART_SLOTS + (half or 0) * (PART_SLOTS // 2), PART_SLOTS // (1 if half is None else 2)),
        pl.ds(0, SPLIT),
    ], peers)
    shares = Reduce(
        copy,
        halves_at(part, 0, PART_SLOTS, 0, SPLIT_BACK),
        (d_relay_a, d_full_a, d_across_a, d_across_b, d_relay_b, d_full_b),
        peers,
    )
    wide_backs = []
    for group in range(4):
        copies = []
        for dz, dy in hops:
            e_to, y_to, k_to = exchange(dz, dy)
            copies.append(
                copy(
                    part.at[
                        pl.ds(2 * group, 2),
                        pl.ds(pl.multiple_of(dz * PART_SLOTS + y_to * CAP, CAP), CAP),
                        pl.ds(SPLIT_BACK, D - SPLIT_BACK),
                    ],
                    wide_back.at[pl.ds(2 * group, 2), own_slots],
                    (pipe, e_to, k_to),
                )
            )
        wide_backs.append(copies)

    for one in sends:
        one.wait_recv()
    dispatch.step(0)
    for one in loads[5:]:
        one.wait()

    def expert(group, carry):
        for number in range(4):

            @pl.when(group == number)
            def _(number=number):
                dispatch.step(number + 1)
                for one in wide_sends[number]:
                    one.wait_recv()
                if number == 3:
                    shares.early()

        places = pl.ds(group * 2, 2)

        def hidden(n, inner):
            columns = pl.ds(pl.multiple_of(n * 512, 512), 512)
            block = rows[places].reshape(2 * SLOTS, D)
            gate = jnp.dot(block, wg[:, columns], preferred_element_type=F32)
            upper = jnp.dot(block, wu[:, columns], preferred_element_type=F32)
            act[:, columns] = (gate / (1.0 + jnp.exp(-gate)) * upper).astype(BF)
            return inner

        lax.fori_loop(0, HID // 512, hidden, 0)

        def down(n, inner):
            columns = pl.ds(pl.multiple_of(n * 512, 512), 512)
            block = jnp.dot(act[...], wd[:, columns], preferred_element_type=F32).astype(BF)
            part[places, :, columns] = block.reshape(2, SLOTS, 512)
            return inner

        lax.fori_loop(0, D // 512, down, 0)
        for number in range(4):

            @pl.when(group == number)
            def _(number=number):
                for one in wide_backs[number]:
                    one.start()
                for place in (2 * number, 2 * number + 1):
                    wide_back[place, own_slots, :] = part[place, own_block, SPLIT_BACK:]

        return carry

    lax.fori_loop(0, 4, expert, 0)

    sums = Reduce(
        copy,
        halves_at(moe, 0, 16, 0, D - SPLIT_BACK),
        (m_relay_a, m_full_a, m_across_a, m_across_b, m_relay_b, m_full_b),
        peers,
    )
    narrow, wide = shares.run(), sums.run()
    for _ in range(4):
        next(narrow)
    for group in range(4):
        for one in wide_backs[group]:
            one.wait_recv()
        for place in (2 * group, 2 * group + 1):
            moe[place] = combined(place, wide_back[place]).astype(BF)
    sums.early()
    next(wide)
    next(narrow)
    next(wide)
    next(wide)
    next(narrow)
    for _ in range(3):
        next(wide)
    for _ in narrow:
        pass
    sum_a, sum_b = shares.sums
    final[0:PART_SLOTS, :] = sum_a.astype(BF)
    final[PART_SLOTS:, :] = sum_b.astype(BF)

    backs = []
    for dz, dy in hops:
        e_to, y_to, k_to = exchange(dz, dy)
        backs.append(
            copy(
                final.at[pl.ds(pl.multiple_of(dz * PART_SLOTS + y_to * CAP, CAP), CAP)],
                returned.at[own_slots],
                (pipe, e_to, k_to),
            )
        )
        backs[-1].start()
    returned[own_slots, :] = final[own_block, :]
    for _ in wide:
        pass
    sum_a, sum_b = sums.sums
    handed[0:16, SPLIT_BACK:] = (state[0:16, SPLIT_BACK:] + sum_a).astype(BF)
    handed[16:32, SPLIT_BACK:] = (state[16:32, SPLIT_BACK:] + sum_b).astype(BF)
    for one in backs:
        one.wait_recv()
    handed[:, :SPLIT_BACK] = (state[:, :SPLIT_BACK] + combined(OWN, returned[...])).astype(BF)
    handing = copy(handed, out_ref, other_core)
    handing.start()
    for one in (features, attention, spread, dispatch, shares, sums):
        one.finish()
    for one in sum(wide_sends + wide_backs, sends + backs):
        one.wait_send()
    handing.wait()


def buffers(part_rows, width):
    return [
        pltpu.VMEM((4, part_rows, width // 2), BF),
        pltpu.VMEM((4, part_rows, width), BF),
        pltpu.VMEM((part_rows, width), BF),
        pltpu.VMEM((4, part_rows, width), BF),
        pltpu.VMEM((2, part_rows, width // 2), BF),
        pltpu.VMEM((2, part_rows, width), BF),
    ]


def on_device(
    inputs,
    attn_gain,
    query_weight,
    key_weight,
    value_weight,
    out_weight,
    ffn_gain,
    gate_weight,
    up_weight,
    down_weight,
    expert_ids,
    route_weights,
):
    cosine, sine = rope_tables()
    anywhere = pl.BlockSpec(memory_space=pl.ANY)
    vmem = pl.BlockSpec(memory_space=pltpu.VMEM)
    handed = pl.pallas_call(
        layer,
        out_shape=jax.ShapeDtypeStruct((TOK, D), BF),
        in_specs=[anywhere, vmem] + [anywhere] * 4 + [vmem] + [anywhere] * 3 + [vmem] * 4,
        out_specs=anywhere,
        scratch_shapes=[
            pltpu.VMEM((D, QKV), BF),
            pltpu.VMEM((384, D), BF),
            pltpu.VMEM((D, HID), BF),
            pltpu.VMEM((D, HID), BF),
            pltpu.VMEM((HID, D), BF),
            pltpu.VMEM((8, X_ROWS, COLS), BF),
            pltpu.VMEM((SEQ, QKV), F32),
            pltpu.VMEM((SEQ, QKV), BF),
            pltpu.VMEM((SEQ, 384), BF),
            pltpu.VMEM((SEQ, D), BF),
            pltpu.VMEM((TOK, D), F32),
            pltpu.VMEM((8, SLOTS, TOK), BF),
            pltpu.VMEM((2, 8, SLOTS, TOK), BF),
            pltpu.VMEM((SLOTS, SPLIT), BF),
            pltpu.VMEM((8, TOK, D - SPLIT), BF),
            pltpu.VMEM((8, 8, CAP, D - SPLIT), BF),
            pltpu.VMEM((8, SLOTS, D), BF),
            pltpu.VMEM((2 * SLOTS, HID), BF),
            pltpu.VMEM((8, SLOTS, D), BF),
            pltpu.VMEM((SLOTS, SPLIT_BACK), BF),
            pltpu.VMEM((SLOTS, SPLIT_BACK), BF),
            pltpu.VMEM((8, SLOTS, D - SPLIT_BACK), BF),
            pltpu.VMEM((8, TOK, D - SPLIT_BACK), BF),
            pltpu.VMEM((TOK, D), BF),
            *buffers(16, D),
            *buffers(PART_SLOTS, SPLIT_BACK),
            *buffers(16, D - SPLIT_BACK),
            pltpu.SemaphoreType.DMA((8,)),
            pltpu.SemaphoreType.DMA((174,)),
            pltpu.SemaphoreType.DMA((174,)),
        ],
        compiler_params=pltpu.CompilerParams(
            collective_id=0, has_side_effects=True, vmem_limit_bytes=60 * 2**20
        ),
        cost_estimate=pl.CostEstimate(flops=22_000_000_000, bytes_accessed=26_000_000, transcendentals=0),
        name="layer",
    )(
        inputs[0],
        attn_gain,
        query_weight[0],
        key_weight[0],
        value_weight[0],
        out_weight[0],
        ffn_gain,
        gate_weight[0, 0],
        up_weight[0, 0],
        down_weight[0, 0],
        expert_ids[0].T,
        route_weights[0].T,
        jnp.asarray(cosine),
        jnp.asarray(sine),
    )
    return handed[None]


def solution(mesh):
    in_specs = (
        P("pipe", "exp", "etp"),
        P("pipe", None),
        P("pipe", None, "etp"),
        P("pipe", None, "etp"),
        P("pipe", None, "etp"),
        P("pipe", "etp", None),
        P("pipe", None),
        P("pipe", "exp", None, "etp"),
        P("pipe", "exp", None, "etp"),
        P("pipe", "exp", "etp", None),
        P("pipe", ("exp", "etp"), None),
        P("pipe", ("exp", "etp"), None),
    )
    out_specs = P("pipe", ("exp", "etp"), None)
    return jax.shard_map(
        on_device, mesh=mesh, in_specs=in_specs, out_specs=out_specs, check_vma=False
    )
```

```python
import jax
import jax.numpy as jnp
import numpy as np
from jax import lax
from jax.experimental import pallas as pl
from jax.experimental.pallas import tpu as pltpu
from jax.sharding import PartitionSpec as P

D = 3072
HQ = 24
HK = 8
HD = 128
CAP = 16
SEQ = 256
TOK = 32
COLS = D // 8
QKV = 640
HID = 1024

epsilon = 1e-05
rope_base = 1000000.0

MESH = pl.DeviceIdType.MESH
BF = jnp.bfloat16
F32 = jnp.float32

OWN, Z, L, R, LZ, RZ, O, OZ = range(8)
SLOTS = 8 * CAP
HALF_SLOTS = SLOTS // 2
SPLIT = 2048
SPLIT_BACK = 2048
PROJ_CUT = 1664
TOKENS_CUT = 640
SPLIT_CUT = 1152
BACK_CUT = 1152
MOE_CUT = 640
META = 16
X_ROWS = SEQ + META


def rope_tables():
    half = HD // 2
    angles = np.arange(SEQ)[:, None] * rope_base ** (-np.arange(half) / half)[None, :]
    cosine, sine = np.cos(angles), np.sin(angles)
    return (
        np.concatenate([cosine, cosine], axis=1).astype(np.float32),
        np.concatenate([-sine, sine], axis=1).astype(np.float32),
    )


class Gather:
    def __init__(self, copy, at, peers):
        left, right, across = peers

        def plan(place, part, half, device, there):
            return lambda: copy(at(place, part, half), at(there, part, half), device)

        steps = {
            "a_z": plan(OWN, 0, None, across, Z),
            "a_l": plan(OWN, 0, None, left, R),
            "a_r": plan(OWN, 0, None, right, L),
            "b_z": plan(OWN, 1, None, across, Z),
            "b_l": plan(OWN, 1, None, left, R),
            "b_r": plan(OWN, 1, None, right, L),
            "za_l": plan(Z, 0, None, left, RZ),
            "za_r": plan(Z, 0, None, right, LZ),
            "lb_r": plan(L, 1, 0, right, O),
            "rb_l": plan(R, 1, 1, left, O),
            "lb_z": plan(L, 1, None, across, LZ),
            "rb_z": plan(R, 1, None, across, RZ),
            "la_r": plan(L, 0, 0, right, O),
            "ra_l": plan(R, 0, 1, left, O),
            "lza_r": plan(LZ, 0, 0, right, OZ),
            "rza_l": plan(RZ, 0, 1, left, OZ),
            "ob_z": plan(O, 1, None, across, OZ),
        }
        self.copies = {name: make() for name, make in steps.items()}

    def start(self, *names):
        for name in names:
            self.copies[name].start()

    def arrive(self, *names):
        for name in names:
            self.copies[name].wait_recv()

    def step(self, number):
        if number == 0:
            self.start("b_r", "b_l", "a_z", "a_r", "a_l", "b_z")
        if number == "part 0":
            self.start("a_z", "a_r", "a_l")
        if number == "part 1":
            self.start("b_r", "b_l", "b_z")
        if number == 1:
            self.arrive("b_r")
            self.start("lb_r", "lb_z")
            self.arrive("b_l")
            self.start("rb_l", "rb_z")
            self.arrive("a_z")
            self.start("za_r", "za_l")
            self.arrive("b_z")
        if number == 2:
            self.arrive("a_r", "a_l")
            self.start("la_r", "ra_l")
            self.arrive("lb_r", "rb_l")
            self.start("ob_z")
        if number == 3:
            self.arrive("za_r", "za_l")
            self.start("lza_r", "rza_l")
            self.arrive("lb_z", "rb_z")
        if number == 4:
            self.arrive("la_r", "ra_l", "lza_r", "rza_l", "ob_z")

    def finish(self):
        for one in self.copies.values():
            one.wait_send()


class Reduce:
    def __init__(self, copy, at, buffers, peers):
        left, right, across = peers
        self.at = at
        self.relay_a, self.full_a, self.across_a, self.across_b, self.relay_b, self.full_b = buffers

        def halved(ref, i, half):
            count = ref.shape[1] // 2
            return ref.at[i, pl.ds(half * count, count)]

        self.copies = {
            "oz_r": copy(at(OZ, 0, 0), self.relay_a.at[2], right),
            "oz_l": copy(at(OZ, 0, 1), self.relay_a.at[3], left),
            "o_r": copy(at(O, 0, 0), self.relay_a.at[0], right),
            "o_l": copy(at(O, 0, 1), self.relay_a.at[1], left),
            "z_z": copy(at(Z, 0, None), self.across_a, across),
            "b_own": copy(at(Z, 1, None), self.across_b.at[0], across),
            "b_left": copy(at(LZ, 1, None), self.across_b.at[1], across),
            "b_right": copy(at(RZ, 1, None), self.across_b.at[2], across),
            "b_opp": copy(at(OZ, 1, None), self.across_b.at[3], across),
            "bo_r": copy(at(O, 1, 0), self.relay_b.at[0], right),
            "bo_l": copy(at(O, 1, 1), self.relay_b.at[1], left),
        }
        for half in (0, 1):
            self.copies["rz%d" % half] = copy(at(RZ, 0, half), halved(self.full_a, 2, half), right)
            self.copies["lz%d" % half] = copy(at(LZ, 0, half), halved(self.full_a, 3, half), left)
            self.copies["r%d" % half] = copy(at(R, 0, half), halved(self.full_a, 0, half), right)
            self.copies["l%d" % half] = copy(at(L, 0, half), halved(self.full_a, 1, half), left)
            self.copies["br%d" % half] = copy(at(R, 1, half), halved(self.full_b, 0, half), right)
            self.copies["bl%d" % half] = copy(at(L, 1, half), halved(self.full_b, 1, half), left)

    def start(self, *names):
        for name in names:
            self.copies[name].start()

    def arrive(self, *names):
        for name in names:
            self.copies[name].wait_recv()

    def add(self, place, part, half, *terms):
        ref = self.at(place, part, half)
        total = ref[...].astype(F32)
        for term in terms:
            total = total + term[...].astype(F32)
        ref[...] = total.astype(BF)

    def total(self, part, *terms):
        result = self.at(OWN, part, None)[...].astype(F32)
        for term in terms:
            result = result + term.astype(F32)
        return result

    def near(self):
        self.start("r1", "l0", "b_own")

    def middle(self):
        self.start("rz1", "lz0", "b_left")

    def far(self):
        self.start("oz_r", "oz_l", "b_opp", "o_r", "o_l", "b_right")

    def run(self):
        self.arrive("oz_r")
        self.add(RZ, 0, 0, self.relay_a.at[2])
        self.start("rz0")
        self.arrive("oz_l")
        self.add(LZ, 0, 1, self.relay_a.at[3])
        self.start("lz1")
        yield
        self.arrive("b_opp")
        self.add(O, 1, None, self.across_b.at[3])
        self.start("bo_r", "bo_l")
        yield
        self.arrive("o_r")
        self.add(R, 0, 0, self.relay_a.at[0])
        self.start("r0")
        self.arrive("o_l")
        self.add(L, 0, 1, self.relay_a.at[1])
        self.start("l1")
        yield
        self.arrive("rz0", "rz1", "lz0", "lz1")
        self.add(Z, 0, None, self.full_a.at[2], self.full_a.at[3])
        self.start("z_z")
        yield
        self.arrive("b_right")
        self.add(R, 1, None, self.across_b.at[2])
        self.start("br1")
        self.arrive("b_left")
        self.add(L, 1, None, self.across_b.at[1])
        self.start("bl0")
        yield
        self.arrive("bo_r")
        self.add(R, 1, 0, self.relay_b.at[0])
        self.start("br0")
        self.arrive("bo_l")
        self.add(L, 1, 1, self.relay_b.at[1])
        self.start("bl1")
        yield
        self.arrive("r0", "r1", "l0", "l1", "z_z")
        self.sum_a = self.total(0, self.full_a[0], self.full_a[1], self.across_a[...])
        yield
        self.arrive("b_own", "br0", "br1", "bl0", "bl1")
        self.sum_b = self.total(1, self.across_b[0], self.full_b[0], self.full_b[1])

    def finish(self):
        for one in self.copies.values():
            one.wait_send()


def placed(first_ids, second_ids):
    slot_row = lax.broadcasted_iota(jnp.int32, (SLOTS, TOK), 0)
    expert = (slot_row // CAP).astype(F32)
    first_route = (first_ids == expert).astype(F32)
    second_route = (second_ids == expert).astype(F32)
    earlier = (
        lax.broadcasted_iota(jnp.int32, (TOK, TOK), 0) < lax.broadcasted_iota(jnp.int32, (TOK, TOK), 1)
    ).astype(BF)
    before = jnp.dot((first_route + second_route).astype(BF), earlier, preferred_element_type=F32)
    here = (before == (slot_row % CAP).astype(F32)).astype(F32)
    return first_route * here, second_route * here


def split_in_three(values):
    high = values.astype(BF).astype(F32)
    middle = (values - high).astype(BF).astype(F32)
    return high, middle, values - high - middle


def layer(
    x_ref, gain1_hbm, wq_ref, wk_ref, wv_ref, wo_ref, gain2_hbm, wg_ref, wu_ref, wd_ref, ids_hbm, weights_hbm,
    cos_hbm, sin_hbm, out_ref,
    ids_ref, weights_ref, gain1_ref, gain2_ref, cos_ref, sin_ref,
    wqkv, wo, wg, wu, wd, xs, acc, heads, mixed, proj, state, tables, combine, outgoing, tokens, wide_out, rows, act,
    part, final, returned, wide_back, moe, state_out, state_other, state_wide, meta_other,
    p_relay_a, p_full_a, p_across_a, p_across_b, p_relay_b, p_full_b,
    d_relay_a, d_full_a, d_across_a, d_across_b, d_relay_b, d_full_b,
    m_relay_a, m_full_a, m_across_a, m_across_b, m_relay_b, m_full_b,
    load_sem, send_sem, recv_sem,
):
    pipe, exp, etp = lax.axis_index("pipe"), lax.axis_index("exp"), lax.axis_index("etp")
    zh, y = exp // 4, exp % 4
    zl, x = etp // 4, etp % 4

    def ring(zl_to, step):
        return zl_to * 4 + (x + step) % 4

    index_of = {
        OWN: etp, Z: ring(1 - zl, 0), L: ring(zl, 3), R: ring(zl, 1),
        LZ: ring(1 - zl, 3), RZ: ring(1 - zl, 1), O: ring(zl, 2), OZ: ring(1 - zl, 2),
    }
    peers = tuple((pipe, exp, index_of[place]) for place in (L, R, Z))

    def exchange(dz, dy):
        zh_to, y_to = (zh + dz) % 2, (y + dy) % 4
        return zh_to * 4 + y_to, y_to, (etp if dz == 0 else index_of[Z])

    hops = [(dz, dy) for dy in (2, 1, 3, 0) for dz in (1, 0) if (dz, dy) != (0, 0)]
    other_core = (1 - pipe, exp, etp)

    barrier = pltpu.get_barrier_semaphore()
    for device in peers:
        pl.semaphore_signal(barrier, inc=1, device_id=device, device_id_type=MESH)
    for dz, dy in hops:
        e_to, _, k_to = exchange(dz, dy)
        for section in (pipe, 1 - pipe):
            pl.semaphore_signal(barrier, inc=1, device_id=(section, e_to, k_to), device_id_type=MESH)
    pl.semaphore_signal(barrier, inc=1, device_id=other_core, device_id_type=MESH)

    loads = [
        pltpu.make_async_copy(source, target, load_sem.at[i])
        for i, (source, target) in enumerate(
            (
                (ids_hbm, ids_ref),
                (weights_hbm, weights_ref),
                (x_ref, xs.at[0, pl.ds(0, SEQ)]),
                (gain1_hbm, gain1_ref),
                (wq_ref, wqkv.at[:, pl.ds(0, 384)]),
                (wk_ref, wqkv.at[:, pl.ds(384, 128)]),
                (wv_ref, wqkv.at[:, pl.ds(512, 128)]),
                (cos_hbm, cos_ref),
                (sin_hbm, sin_ref),
                (wo_ref, wo),
                (gain2_hbm, gain2_ref),
                (wg_ref, wg),
                (wu_ref, wu),
                (wd_ref, wd),
            )
        )
    ]
    for one in loads:
        one.start()

    for one in loads[:2]:
        one.wait()
    xs[0, SEQ:X_ROWS, :] = jnp.zeros((META, COLS), BF)
    meta_row = lax.broadcasted_iota(jnp.int32, (META, TOK), 0)
    meta_rows = [ids_ref[0:1, :].astype(F32), ids_ref[1:2, :].astype(F32)]
    meta_rows += [*split_in_three(weights_ref[0:1, :]), *split_in_three(weights_ref[1:2, :])]
    meta = jnp.zeros((META, TOK), F32)
    for i, row in enumerate(meta_rows):
        meta = jnp.where(meta_row == i, row, meta)
    xs[0, SEQ:X_ROWS, 0:TOK] = meta.astype(BF)
    loads[2].wait()
    pl.semaphore_wait(barrier, 4 + 2 * len(hops))

    used = [0]

    def copy(source, target, device):
        i = used[0]
        used[0] = i + 1
        return pltpu.make_async_remote_copy(
            src_ref=source, dst_ref=target, send_sem=send_sem.at[i], recv_sem=recv_sem.at[i],
            device_id=device, device_id_type=MESH,
        )

    x_parts = {
        (0, None): (0, 144), (0, 0): (0, 80), (0, 1): (80, 64),
        (1, None): (144, 128), (1, 0): (144, 64), (1, 1): (208, 64),
    }

    def xs_at(place, part_no, half):
        return xs.at[place, pl.ds(*x_parts[part_no, half])]

    features = Gather(copy, xs_at, peers)
    squares = []

    def project(place):
        offset = pl.multiple_of(index_of[place] * COLS, 128)
        block = xs[place, 0:SEQ, :].astype(F32)
        squares.append(jnp.sum(block * block, axis=1, keepdims=True))
        scaled = (block * gain1_ref[:, pl.ds(offset, COLS)].astype(F32)).astype(BF)
        term = jnp.dot(scaled, wqkv[pl.ds(offset, COLS), :], preferred_element_type=F32)
        acc[...] = term if place == OWN else acc[...] + term
        own_rows = pl.ds(pl.multiple_of(etp * TOK, TOK), TOK)
        state[:, pl.ds(offset, COLS)] = xs[place, own_rows, :].astype(F32)

    features.step(0)
    meta_copy = copy(xs.at[OWN, pl.ds(SEQ, META)], meta_other, other_core)
    meta_copy.start()
    for one in loads[3:7]:
        one.wait()
    project(OWN)
    features.step(1)
    features.step(2)
    for place in (Z, L, R):
        project(place)
    features.step(3)
    for place in (LZ, RZ):
        project(place)
    features.step(4)
    for place in (O, OZ):
        project(place)

    for one in loads[7:11]:
        one.wait()
    factor = lax.rsqrt(sum(squares) * (1.0 / D) + epsilon)
    for i in range(5):
        block = acc[:, i * HD : (i + 1) * HD] * factor
        if i < 4:
            block = block * cos_ref[...] + pltpu.roll(block, HD // 2, 1) * sin_ref[...]
        heads[:, i * HD : (i + 1) * HD] = block.astype(BF)
    causal = lax.broadcasted_iota(jnp.int32, (SEQ, SEQ), 0) >= lax.broadcasted_iota(jnp.int32, (SEQ, SEQ), 1)
    keys, values = heads[:, 384:512], heads[:, 512:640]
    for i in range(3):
        scores = lax.dot_general(
            heads[:, i * HD : (i + 1) * HD], keys, (((1,), (1,)), ((), ())), preferred_element_type=F32
        ) * HD ** (-0.5)
        scores = jnp.where(causal, scores, -1e30)
        expo = jnp.exp(scores - jnp.max(scores, axis=1, keepdims=True))
        probs = (expo / jnp.sum(expo, axis=1, keepdims=True)).astype(BF)
        mixed[:, i * HD : (i + 1) * HD] = jnp.dot(probs, values, preferred_element_type=F32).astype(BF)

    def out_columns(n, carry):
        columns = pl.ds(pl.multiple_of(n * 512, 512), 512)
        proj[:, columns] = jnp.dot(mixed[...], wo[:, columns], preferred_element_type=F32).astype(BF)
        return carry

    lax.fori_loop(0, D // 512, out_columns, 0)

    def cut_at(block_of, count, cut, width):
        def at(place, part_no, half):
            ref, first = block_of(place)
            rows_here = pl.ds(first, count)
            if half is not None:
                rows_here = pl.ds(first + half * (count // 2), count // 2)
            return ref.at[rows_here, pl.ds(0, cut) if part_no == 0 else pl.ds(cut, width - cut)]

        return at

    def proj_block(place):
        return proj, pl.multiple_of(index_of[place] * TOK, TOK)

    proj_at = cut_at(proj_block, TOK, PROJ_CUT, D)

    attention = Reduce(
        copy, proj_at, (p_relay_a, p_full_a, p_across_a, p_across_b, p_relay_b, p_full_b), peers
    )
    attention.far()
    attention.middle()
    attention.near()
    running = attention.run()

    def routes(sent):
        first_route, second_route = placed(sent[0:1], sent[1:2])
        weight = first_route * (sent[2:3] + sent[3:4] + sent[4:5])
        weight = weight + second_route * (sent[5:6] + sent[6:7] + sent[7:8])
        return first_route + second_route, weight

    for place in range(8):
        table, weight = routes(xs[place, SEQ:X_ROWS, 0:TOK].astype(F32))
        tables[place] = table.astype(BF)
        high = weight.astype(BF)
        combine[0, place] = high
        combine[1, place] = (weight - high.astype(F32)).astype(BF)

    def combined(high, low, outputs):
        over_slots = (((0,), (0,)), ((), ()))
        total = lax.dot_general(high, outputs, over_slots, preferred_element_type=F32)
        return total + lax.dot_general(low, outputs, over_slots, preferred_element_type=F32)

    for _ in running:
        pass
    state[:, PROJ_CUT:] = (state[:, PROJ_CUT:] + attention.sum_b).astype(BF).astype(F32)
    state[:, :PROJ_CUT] = (state[:, :PROJ_CUT] + attention.sum_a).astype(BF).astype(F32)
    state_now = state[...]
    factor2 = lax.rsqrt(jnp.mean(state_now * state_now, axis=1, keepdims=True) + epsilon)
    ffn_in = (state_now * factor2 * gain2_ref[...].astype(F32)).astype(BF)

    tokens[OWN] = ffn_in[:, SPLIT:]

    spread = Gather(copy, cut_at(lambda place: (tokens.at[place], 0), TOK, TOKENS_CUT, D - SPLIT), peers)
    spread.step(0)

    outgoing[...] = jnp.dot(tables[OWN], ffn_in[:, :SPLIT], preferred_element_type=F32).astype(BF)
    sends = []
    for columns in (pl.ds(SPLIT_CUT, SPLIT - SPLIT_CUT), pl.ds(0, SPLIT_CUT)):
        copies = []
        for dz, dy in hops:
            e_to, _, k_to = exchange(dz, dy)
            copies.append(
                copy(
                    outgoing.at[pl.ds(pl.multiple_of(e_to * CAP, CAP), CAP), columns],
                    rows.at[OWN, pl.ds(pl.multiple_of(dz * HALF_SLOTS + y * CAP, CAP), CAP), columns],
                    (pipe, e_to, k_to),
                )
            )
            copies[-1].start()
        sends.append(copies)
    own_slots = pl.ds(pl.multiple_of(exp * CAP, CAP), CAP)
    own_block = pl.ds(pl.multiple_of(y * CAP, CAP), CAP)
    rows[OWN, own_block, 0:SPLIT] = outgoing[own_slots, :]

    wide_sends = []

    def widen(group):
        for place in (2 * group, 2 * group + 1):
            block = jnp.dot(tables[place], tokens[place], preferred_element_type=F32).astype(BF)
            wide_out[:, place] = block.reshape(8, CAP, D - SPLIT)
        copies = []
        for dz, dy in hops:
            e_to, _, k_to = exchange(dz, dy)
            copies.append(
                copy(
                    wide_out.at[e_to, pl.ds(2 * group, 2)],
                    rows.at[
                        pl.ds(2 * group, 2),
                        pl.ds(pl.multiple_of(dz * HALF_SLOTS + y * CAP, CAP), CAP),
                        pl.ds(SPLIT, D - SPLIT),
                    ],
                    (pipe, e_to, k_to),
                )
            )
            copies[-1].start()
        for place in (2 * group, 2 * group + 1):
            rows[place, own_block, SPLIT:] = wide_out[exp, place]
        wide_sends.append(copies)

    dispatch = Gather(copy, cut_at(lambda place: (rows.at[place], 0), SLOTS, SPLIT_CUT, SPLIT), peers)
    shares = Reduce(
        copy,
        cut_at(lambda place: (part.at[place], 0), SLOTS, BACK_CUT, SPLIT_BACK),
        (d_relay_a, d_full_a, d_across_a, d_across_b, d_relay_b, d_full_b),
        peers,
    )
    narrow = shares.run()

    spread.step(1)
    widen(0)
    spread.step(2)
    for one in sends[0]:
        one.wait_recv()
    dispatch.step("part 1")
    widen(1)
    spread.step(3)
    widen(2)
    for one in sends[1]:
        one.wait_recv()
    dispatch.step("part 0")
    spread.step(4)
    widen(3)
    state_out[...] = state[:, :SPLIT_BACK].astype(BF)
    state_copy = copy(state_out, state_other, other_core)
    state_copy.start()

    wide_backs = []
    for group in range(4):
        copies = []
        for dz, dy in hops:
            e_to, y_to, k_to = exchange(dz, dy)
            copies.append(
                copy(
                    part.at[
                        pl.ds(2 * group, 2),
                        pl.ds(pl.multiple_of(dz * HALF_SLOTS + y_to * CAP, CAP), CAP),
                        pl.ds(SPLIT_BACK, D - SPLIT_BACK),
                    ],
                    wide_back.at[pl.ds(2 * group, 2), own_slots],
                    (pipe, e_to, k_to),
                )
            )
        wide_backs.append(copies)

    for one in loads[11:]:
        one.wait()

    def expert(group, carry):
        for number in range(4):

            @pl.when(group == number)
            def _(number=number):
                if number == 3:
                    shares.middle()
                dispatch.step(number + 1)
                if number == 2:
                    shares.near()
                for one in wide_sends[number]:
                    one.wait_recv()

        places = pl.ds(group * 2, 2)

        block = rows[places].reshape(2 * SLOTS, D)
        gate = jnp.dot(block, wg[...], preferred_element_type=F32)
        upper = jnp.dot(block, wu[...], preferred_element_type=F32)
        act[...] = (gate / (1.0 + jnp.exp(-gate)) * upper).astype(BF)

        def down(n, inner):
            columns = pl.ds(pl.multiple_of(n * 1024, 1024), 1024)
            block = jnp.dot(act[...], wd[:, columns], preferred_element_type=F32).astype(BF)
            part[places, :, columns] = block.reshape(2, SLOTS, 1024)
            return inner

        lax.fori_loop(0, -(-SPLIT_BACK // 1024), down, 0)

        @pl.when(group == 3)
        def _():
            shares.far()

        lax.fori_loop(-(-SPLIT_BACK // 1024), D // 1024, down, 0)
        for number in range(4):

            @pl.when(group == number)
            def _(number=number):
                for one in wide_backs[number]:
                    one.start()
                for place in (2 * number, 2 * number + 1):
                    wide_back[place, own_slots, :] = part[place, own_block, SPLIT_BACK:]

        return carry

    lax.fori_loop(0, 4, expert, 0)

    sums = Reduce(
        copy,
        cut_at(lambda place: (moe.at[place], 0), TOK, MOE_CUT, D - SPLIT_BACK),
        (m_relay_a, m_full_a, m_across_a, m_across_b, m_relay_b, m_full_b),
        peers,
    )
    wide = sums.run()
    for _ in range(3):
        next(narrow)
    for group in range(4):
        for one in wide_backs[group]:
            one.wait_recv()
        for place in (2 * group, 2 * group + 1):
            moe[place] = combined(combine[0, place], combine[1, place], wide_back[place]).astype(BF)
    sums.far()
    sums.middle()
    sums.near()
    next(narrow)
    for _ in range(3):
        next(wide)
    next(narrow)
    next(wide)
    next(narrow)
    for _ in range(2):
        next(wide)

    backs = []

    def send_back(columns):
        copies = []
        for dz, dy in hops + [(0, 0)]:
            e_to, y_to, k_to = exchange(dz, dy)
            copies.append(
                copy(
                    final.at[pl.ds(pl.multiple_of(dz * HALF_SLOTS + y_to * CAP, CAP), CAP), columns],
                    returned.at[own_slots, columns],
                    (1 - pipe, e_to, k_to),
                )
            )
            copies[-1].start()
        backs.append(copies)

    meta_copy.wait_recv()
    _, weight = routes(meta_other[:, 0:TOK].astype(F32))
    high = weight.astype(BF)
    low = (weight - high.astype(F32)).astype(BF)
    next(narrow)
    final[:, :BACK_CUT] = shares.sum_a.astype(BF)
    send_back(pl.ds(0, BACK_CUT))
    next(wide)
    for _ in narrow:
        pass
    final[:, BACK_CUT:] = shares.sum_b.astype(BF)
    send_back(pl.ds(BACK_CUT, SPLIT_BACK - BACK_CUT))
    for _ in wide:
        pass
    border = SPLIT_BACK + MOE_CUT
    state_wide[:, MOE_CUT:] = (state[:, border:] + sums.sum_b).astype(BF)
    state_wide[:, :MOE_CUT] = (state[:, SPLIT_BACK:border] + sums.sum_a).astype(BF)
    wide_copy = copy(state_wide, out_ref.at[:, pl.ds(SPLIT_BACK, D - SPLIT_BACK)], other_core)
    wide_copy.start()
    state_copy.wait_recv()
    for copies, columns in zip(backs, (slice(0, BACK_CUT), slice(BACK_CUT, SPLIT_BACK))):
        for one in copies:
            one.wait_recv()
        total = state_other[:, columns].astype(F32) + combined(high, low, returned[:, columns])
        out_ref[:, columns] = total.astype(BF)
    for one in (features, attention, spread, dispatch, shares, sums):
        one.finish()
    for one in sum(sends + wide_sends + wide_backs + backs, [meta_copy, state_copy]):
        one.wait_send()
    wide_copy.wait()


def buffers(rows, cut, width):
    rest = width - cut
    return [
        pltpu.VMEM((4, rows // 2, cut), BF),
        pltpu.VMEM((4, rows, cut), BF),
        pltpu.VMEM((rows, cut), BF),
        pltpu.VMEM((4, rows, rest), BF),
        pltpu.VMEM((2, rows // 2, rest), BF),
        pltpu.VMEM((2, rows, rest), BF),
    ]


def on_device(
    inputs,
    attn_gain,
    query_weight,
    key_weight,
    value_weight,
    out_weight,
    ffn_gain,
    gate_weight,
    up_weight,
    down_weight,
    expert_ids,
    route_weights,
):
    cosine, sine = rope_tables()
    anywhere = pl.BlockSpec(memory_space=pl.ANY)
    handed = pl.pallas_call(
        layer,
        out_shape=jax.ShapeDtypeStruct((TOK, D), BF),
        in_specs=[anywhere] * 14,
        out_specs=pl.BlockSpec(memory_space=pltpu.VMEM),
        scratch_shapes=[
            pltpu.VMEM((2, TOK), jnp.int32),
            pltpu.VMEM((2, TOK), F32),
            pltpu.VMEM((1, D), BF),
            pltpu.VMEM((1, D), BF),
            pltpu.VMEM((SEQ, HD), F32),
            pltpu.VMEM((SEQ, HD), F32),
            pltpu.VMEM((D, QKV), BF),
            pltpu.VMEM((384, D), BF),
            pltpu.VMEM((D, HID), BF),
            pltpu.VMEM((D, HID), BF),
            pltpu.VMEM((HID, D), BF),
            pltpu.VMEM((8, X_ROWS, COLS), BF),
            pltpu.VMEM((SEQ, QKV), F32),
            pltpu.VMEM((SEQ, QKV), BF),
            pltpu.VMEM((SEQ, 384), BF),
            pltpu.VMEM((SEQ, D), BF),
            pltpu.VMEM((TOK, D), F32),
            pltpu.VMEM((8, SLOTS, TOK), BF),
            pltpu.VMEM((2, 8, SLOTS, TOK), BF),
            pltpu.VMEM((SLOTS, SPLIT), BF),
            pltpu.VMEM((8, TOK, D - SPLIT), BF),
            pltpu.VMEM((8, 8, CAP, D - SPLIT), BF),
            pltpu.VMEM((8, SLOTS, D), BF),
            pltpu.VMEM((2 * SLOTS, HID), BF),
            pltpu.VMEM((8, SLOTS, D), BF),
            pltpu.VMEM((SLOTS, SPLIT_BACK), BF),
            pltpu.VMEM((SLOTS, SPLIT_BACK), BF),
            pltpu.VMEM((8, SLOTS, D - SPLIT_BACK), BF),
            pltpu.VMEM((8, TOK, D - SPLIT_BACK), BF),
            pltpu.VMEM((TOK, SPLIT_BACK), BF),
            pltpu.VMEM((TOK, SPLIT_BACK), BF),
            pltpu.VMEM((TOK, D - SPLIT_BACK), BF),
            pltpu.VMEM((META, COLS), BF),
            *buffers(TOK, PROJ_CUT, D),
            *buffers(SLOTS, BACK_CUT, SPLIT_BACK),
            *buffers(TOK, MOE_CUT, D - SPLIT_BACK),
            pltpu.SemaphoreType.DMA((14,)),
            pltpu.SemaphoreType.DMA((216,)),
            pltpu.SemaphoreType.DMA((216,)),
        ],
        compiler_params=pltpu.CompilerParams(
            collective_id=0, has_side_effects=True, vmem_limit_bytes=60 * 2**20
        ),
        cost_estimate=pl.CostEstimate(flops=22_000_000_000, bytes_accessed=26_000_000, transcendentals=0),
        name="layer",
    )(
        inputs[0],
        attn_gain,
        query_weight[0],
        key_weight[0],
        value_weight[0],
        out_weight[0],
        ffn_gain,
        gate_weight[0, 0],
        up_weight[0, 0],
        down_weight[0, 0],
        expert_ids[0].T,
        route_weights[0].T,
        jnp.asarray(cosine),
        jnp.asarray(sine),
    )
    return handed[None]


def solution(mesh):
    in_specs = (
        P("pipe", "exp", "etp"),
        P("pipe", None),
        P("pipe", None, "etp"),
        P("pipe", None, "etp"),
        P("pipe", None, "etp"),
        P("pipe", "etp", None),
        P("pipe", None),
        P("pipe", "exp", None, "etp"),
        P("pipe", "exp", None, "etp"),
        P("pipe", "exp", "etp", None),
        P("pipe", ("exp", "etp"), None),
        P("pipe", ("exp", "etp"), None),
    )
    out_specs = P("pipe", ("exp", "etp"), None)
    return jax.shard_map(
        on_device, mesh=mesh, in_specs=in_specs, out_specs=out_specs, check_vma=False
    )
```

```python
import jax
import jax.numpy as jnp
import numpy as np
from jax import lax
from jax.experimental import pallas as pl
from jax.experimental.pallas import tpu as pltpu
from jax.sharding import PartitionSpec as P

D = 3072
HQ = 24
HK = 8
HD = 128
CAP = 16
SEQ = 256
TOK = 32
COLS = D // 8
QKV = 640
HID = 1024

epsilon = 1e-05
rope_base = 1000000.0

MESH = pl.DeviceIdType.MESH
BF = jnp.bfloat16
F32 = jnp.float32

OWN, Z, L, R, LZ, RZ, O, OZ = range(8)
SLOTS = 8 * CAP
HALF_SLOTS = SLOTS // 2
SPLIT = 2048
SPLIT_BACK = 2048
PROJ_CUT = 1664
TOKENS_CUT = 640
SPLIT_CUT = 1152
BACK_CUT = 1152
MOE_CUT = 640
META = 16
X_ROWS = SEQ + META


def rope_tables():
    half = HD // 2
    angles = np.arange(SEQ)[:, None] * rope_base ** (-np.arange(half) / half)[None, :]
    cosine, sine = np.cos(angles), np.sin(angles)
    return (
        np.concatenate([cosine, cosine], axis=1).astype(np.float32),
        np.concatenate([-sine, sine], axis=1).astype(np.float32),
    )


class Gather:
    def __init__(self, copy, at, peers):
        left, right, across = peers

        def plan(place, part, half, device, there):
            return lambda: copy(at(place, part, half), at(there, part, half), device)

        steps = {
            "a_z": plan(OWN, 0, None, across, Z),
            "a_l": plan(OWN, 0, None, left, R),
            "a_r": plan(OWN, 0, None, right, L),
            "b_z": plan(OWN, 1, None, across, Z),
            "b_l": plan(OWN, 1, None, left, R),
            "b_r": plan(OWN, 1, None, right, L),
            "za_l": plan(Z, 0, None, left, RZ),
            "za_r": plan(Z, 0, None, right, LZ),
            "lb_r": plan(L, 1, 0, right, O),
            "rb_l": plan(R, 1, 1, left, O),
            "lb_z": plan(L, 1, None, across, LZ),
            "rb_z": plan(R, 1, None, across, RZ),
            "la_r": plan(L, 0, 0, right, O),
            "ra_l": plan(R, 0, 1, left, O),
            "lza_r": plan(LZ, 0, 0, right, OZ),
            "rza_l": plan(RZ, 0, 1, left, OZ),
            "ob_z": plan(O, 1, None, across, OZ),
        }
        self.copies = {name: make() for name, make in steps.items()}

    def start(self, *names):
        for name in names:
            self.copies[name].start()

    def arrive(self, *names):
        for name in names:
            self.copies[name].wait_recv()

    def step(self, number):
        if number == 0:
            self.start("b_r", "b_l", "a_z", "a_r", "a_l", "b_z")
        if number == "part 0":
            self.start("a_z", "a_r", "a_l")
        if number == "part 1":
            self.start("b_r", "b_l", "b_z")
        if number == 1:
            self.arrive("b_r")
            self.start("lb_r", "lb_z")
            self.arrive("b_l")
            self.start("rb_l", "rb_z")
            self.arrive("a_z")
            self.start("za_r", "za_l")
            self.arrive("b_z")
        if number == 2:
            self.arrive("a_r", "a_l")
            self.start("la_r", "ra_l")
            self.arrive("lb_r", "rb_l")
            self.start("ob_z")
        if number == 3:
            self.arrive("za_r", "za_l")
            self.start("lza_r", "rza_l")
            self.arrive("lb_z", "rb_z")
        if number == 4:
            self.arrive("la_r", "ra_l", "lza_r", "rza_l", "ob_z")

    def finish(self):
        for one in self.copies.values():
            one.wait_send()


class Reduce:
    def __init__(self, copy, at, buffers, peers):
        left, right, across = peers
        self.at = at
        self.relay_a, self.full_a, self.across_a, self.across_b, self.relay_b, self.full_b = buffers

        def halved(ref, i, half):
            count = ref.shape[1] // 2
            return ref.at[i, pl.ds(half * count, count)]

        self.copies = {
            "oz_r": copy(at(OZ, 0, 0), self.relay_a.at[2], right),
            "oz_l": copy(at(OZ, 0, 1), self.relay_a.at[3], left),
            "o_r": copy(at(O, 0, 0), self.relay_a.at[0], right),
            "o_l": copy(at(O, 0, 1), self.relay_a.at[1], left),
            "z_z": copy(at(Z, 0, None), self.across_a, across),
            "b_own": copy(at(Z, 1, None), self.across_b.at[0], across),
            "b_left": copy(at(LZ, 1, None), self.across_b.at[1], across),
            "b_right": copy(at(RZ, 1, None), self.across_b.at[2], across),
            "b_opp": copy(at(OZ, 1, None), self.across_b.at[3], across),
            "bo_r": copy(at(O, 1, 0), self.relay_b.at[0], right),
            "bo_l": copy(at(O, 1, 1), self.relay_b.at[1], left),
        }
        for half in (0, 1):
            self.copies["rz%d" % half] = copy(at(RZ, 0, half), halved(self.full_a, 2, half), right)
            self.copies["lz%d" % half] = copy(at(LZ, 0, half), halved(self.full_a, 3, half), left)
            self.copies["r%d" % half] = copy(at(R, 0, half), halved(self.full_a, 0, half), right)
            self.copies["l%d" % half] = copy(at(L, 0, half), halved(self.full_a, 1, half), left)
            self.copies["br%d" % half] = copy(at(R, 1, half), halved(self.full_b, 0, half), right)
            self.copies["bl%d" % half] = copy(at(L, 1, half), halved(self.full_b, 1, half), left)

    def start(self, *names):
        for name in names:
            self.copies[name].start()

    def arrive(self, *names):
        for name in names:
            self.copies[name].wait_recv()

    def add(self, place, part, half, *terms):
        ref = self.at(place, part, half)
        total = ref[...].astype(F32)
        for term in terms:
            total = total + term[...].astype(F32)
        ref[...] = total.astype(BF)

    def total(self, part, *terms):
        result = self.at(OWN, part, None)[...].astype(F32)
        for term in terms:
            result = result + term.astype(F32)
        return result

    def near(self):
        self.start("r1", "l0", "b_own")

    def middle(self):
        self.start("rz1", "lz0", "b_left")

    def far(self):
        self.start("oz_r", "oz_l", "b_opp", "o_r", "o_l", "b_right")

    def run(self):
        self.arrive("oz_r")
        self.add(RZ, 0, 0, self.relay_a.at[2])
        self.start("rz0")
        self.arrive("oz_l")
        self.add(LZ, 0, 1, self.relay_a.at[3])
        self.start("lz1")
        yield
        self.arrive("b_opp")
        self.add(O, 1, None, self.across_b.at[3])
        self.start("bo_r", "bo_l")
        yield
        self.arrive("o_r")
        self.add(R, 0, 0, self.relay_a.at[0])
        self.start("r0")
        self.arrive("o_l")
        self.add(L, 0, 1, self.relay_a.at[1])
        self.start("l1")
        yield
        self.arrive("rz0", "rz1", "lz0", "lz1")
        self.add(Z, 0, None, self.full_a.at[2], self.full_a.at[3])
        self.start("z_z")
        yield
        self.arrive("b_right")
        self.add(R, 1, None, self.across_b.at[2])
        self.start("br1")
        self.arrive("b_left")
        self.add(L, 1, None, self.across_b.at[1])
        self.start("bl0")
        yield
        self.arrive("bo_r")
        self.add(R, 1, 0, self.relay_b.at[0])
        self.start("br0")
        self.arrive("bo_l")
        self.add(L, 1, 1, self.relay_b.at[1])
        self.start("bl1")
        yield
        self.arrive("r0", "r1", "l0", "l1", "z_z")
        self.sum_a = self.total(0, self.full_a[0], self.full_a[1], self.across_a[...])
        yield
        self.arrive("b_own", "br0", "br1", "bl0", "bl1")
        self.sum_b = self.total(1, self.across_b[0], self.full_b[0], self.full_b[1])

    def finish(self):
        for one in self.copies.values():
            one.wait_send()


def placed(first_ids, second_ids):
    slot_row = lax.broadcasted_iota(jnp.int32, (SLOTS, TOK), 0)
    expert = (slot_row // CAP).astype(F32)
    first_route = (first_ids == expert).astype(F32)
    second_route = (second_ids == expert).astype(F32)
    earlier = (
        lax.broadcasted_iota(jnp.int32, (TOK, TOK), 0) < lax.broadcasted_iota(jnp.int32, (TOK, TOK), 1)
    ).astype(BF)
    before = jnp.dot((first_route + second_route).astype(BF), earlier, preferred_element_type=F32)
    here = (before == (slot_row % CAP).astype(F32)).astype(F32)
    return first_route * here, second_route * here


def split_in_three(values):
    high = values.astype(BF).astype(F32)
    middle = (values - high).astype(BF).astype(F32)
    return high, middle, values - high - middle


def layer(
    x_ref, gain1_hbm, wq_ref, wk_ref, wv_ref, wo_ref, gain2_hbm, wg_ref, wu_ref, wd_ref, ids_hbm, weights_hbm,
    cos_hbm, sin_hbm, out_ref,
    ids_ref, weights_ref, gain1_ref, gain2_ref, cos_ref, sin_ref,
    wqkv, wo, wg, wu, wd, xs, acc, heads, mixed, proj, state, tables, combine, outgoing, tokens, wide_out, rows, act,
    part, final, returned, wide_back, moe, state_out, state_other, state_wide, meta_other,
    p_relay_a, p_full_a, p_across_a, p_across_b, p_relay_b, p_full_b,
    d_relay_a, d_full_a, d_across_a, d_across_b, d_relay_b, d_full_b,
    m_relay_a, m_full_a, m_across_a, m_across_b, m_relay_b, m_full_b,
    load_sem, send_sem, recv_sem,
):
    pipe, exp, etp = lax.axis_index("pipe"), lax.axis_index("exp"), lax.axis_index("etp")
    zh, y = exp // 4, exp % 4
    zl, x = etp // 4, etp % 4

    def ring(zl_to, step):
        return zl_to * 4 + (x + step) % 4

    index_of = {
        OWN: etp, Z: ring(1 - zl, 0), L: ring(zl, 3), R: ring(zl, 1),
        LZ: ring(1 - zl, 3), RZ: ring(1 - zl, 1), O: ring(zl, 2), OZ: ring(1 - zl, 2),
    }
    peers = tuple((pipe, exp, index_of[place]) for place in (L, R, Z))

    def exchange(dz, dy):
        zh_to, y_to = (zh + dz) % 2, (y + dy) % 4
        return zh_to * 4 + y_to, y_to, (etp if dz == 0 else index_of[Z])

    hops = [(dz, dy) for dy in (2, 1, 3, 0) for dz in (1, 0) if (dz, dy) != (0, 0)]
    other_core = (1 - pipe, exp, etp)

    barrier = pltpu.get_barrier_semaphore()
    for device in peers:
        pl.semaphore_signal(barrier, inc=1, device_id=device, device_id_type=MESH)
    for dz, dy in hops:
        e_to, _, k_to = exchange(dz, dy)
        for section in (pipe, 1 - pipe):
            pl.semaphore_signal(barrier, inc=1, device_id=(section, e_to, k_to), device_id_type=MESH)
    pl.semaphore_signal(barrier, inc=1, device_id=other_core, device_id_type=MESH)

    loads = [
        pltpu.make_async_copy(source, target, load_sem.at[i])
        for i, (source, target) in enumerate(
            (
                (ids_hbm, ids_ref),
                (weights_hbm, weights_ref),
                (x_ref, xs.at[0, pl.ds(0, SEQ)]),
                (gain1_hbm, gain1_ref),
                (wq_ref, wqkv.at[:, pl.ds(0, 384)]),
                (wk_ref, wqkv.at[:, pl.ds(384, 128)]),
                (wv_ref, wqkv.at[:, pl.ds(512, 128)]),
                (cos_hbm, cos_ref),
                (sin_hbm, sin_ref),
                (wo_ref, wo),
                (gain2_hbm, gain2_ref),
                (wg_ref, wg),
                (wu_ref, wu),
                (wd_ref, wd),
            )
        )
    ]
    for one in loads:
        one.start()

    for one in loads[:2]:
        one.wait()
    xs[0, SEQ:X_ROWS, :] = jnp.zeros((META, COLS), BF)
    meta_row = lax.broadcasted_iota(jnp.int32, (META, TOK), 0)
    meta_rows = [ids_ref[0:1, :].astype(F32), ids_ref[1:2, :].astype(F32)]
    meta_rows += [*split_in_three(weights_ref[0:1, :]), *split_in_three(weights_ref[1:2, :])]
    meta = jnp.zeros((META, TOK), F32)
    for i, row in enumerate(meta_rows):
        meta = jnp.where(meta_row == i, row, meta)
    xs[0, SEQ:X_ROWS, 0:TOK] = meta.astype(BF)
    loads[2].wait()
    pl.semaphore_wait(barrier, 4 + 2 * len(hops))

    used = [0]

    def copy(source, target, device):
        i = used[0]
        used[0] = i + 1
        return pltpu.make_async_remote_copy(
            src_ref=source, dst_ref=target, send_sem=send_sem.at[i], recv_sem=recv_sem.at[i],
            device_id=device, device_id_type=MESH,
        )

    x_parts = {
        (0, None): (0, 144), (0, 0): (0, 80), (0, 1): (80, 64),
        (1, None): (144, 128), (1, 0): (144, 64), (1, 1): (208, 64),
    }

    def xs_at(place, part_no, half):
        return xs.at[place, pl.ds(*x_parts[part_no, half])]

    features = Gather(copy, xs_at, peers)
    squares = []

    def project(place):
        offset = pl.multiple_of(index_of[place] * COLS, 128)
        block = xs[place, 0:SEQ, :].astype(F32)
        squares.append(jnp.sum(block * block, axis=1, keepdims=True))
        scaled = (block * gain1_ref[:, pl.ds(offset, COLS)].astype(F32)).astype(BF)
        term = jnp.dot(scaled, wqkv[pl.ds(offset, COLS), :], preferred_element_type=F32)
        acc[...] = term if place == OWN else acc[...] + term
        own_rows = pl.ds(pl.multiple_of(etp * TOK, TOK), TOK)
        state[:, pl.ds(offset, COLS)] = xs[place, own_rows, :].astype(F32)

    features.step(0)
    meta_copy = copy(xs.at[OWN, pl.ds(SEQ, META)], meta_other, other_core)
    meta_copy.start()
    for one in loads[3:7]:
        one.wait()
    project(OWN)
    features.step(1)
    features.step(2)
    for place in (Z, L, R):
        project(place)
    features.step(3)
    for place in (LZ, RZ):
        project(place)
    features.step(4)
    for place in (O, OZ):
        project(place)

    for one in loads[7:11]:
        one.wait()
    factor = lax.rsqrt(sum(squares) * (1.0 / D) + epsilon)
    for i in range(5):
        block = acc[:, i * HD : (i + 1) * HD] * factor
        if i < 4:
            block = block * cos_ref[...] + pltpu.roll(block, HD // 2, 1) * sin_ref[...]
        heads[:, i * HD : (i + 1) * HD] = block.astype(BF)
    causal = lax.broadcasted_iota(jnp.int32, (SEQ, SEQ), 0) >= lax.broadcasted_iota(jnp.int32, (SEQ, SEQ), 1)
    keys, values = heads[:, 384:512], heads[:, 512:640]
    for i in range(3):
        scores = lax.dot_general(
            heads[:, i * HD : (i + 1) * HD], keys, (((1,), (1,)), ((), ())), preferred_element_type=F32
        ) * HD ** (-0.5)
        scores = jnp.where(causal, scores, -1e30)
        expo = jnp.exp(scores - jnp.max(scores, axis=1, keepdims=True))
        probs = (expo / jnp.sum(expo, axis=1, keepdims=True)).astype(BF)
        mixed[:, i * HD : (i + 1) * HD] = jnp.dot(probs, values, preferred_element_type=F32).astype(BF)

    def out_columns(n, carry):
        columns = pl.ds(pl.multiple_of(n * 512, 512), 512)
        proj[:, columns] = jnp.dot(mixed[...], wo[:, columns], preferred_element_type=F32).astype(BF)
        return carry

    lax.fori_loop(0, D // 512, out_columns, 0)

    def cut_at(block_of, count, cut, width):
        def at(place, part_no, half):
            ref, first = block_of(place)
            rows_here = pl.ds(first, count)
            if half is not None:
                rows_here = pl.ds(first + half * (count // 2), count // 2)
            return ref.at[rows_here, pl.ds(0, cut) if part_no == 0 else pl.ds(cut, width - cut)]

        return at

    def proj_block(place):
        return proj, pl.multiple_of(index_of[place] * TOK, TOK)

    proj_at = cut_at(proj_block, TOK, PROJ_CUT, D)

    attention = Reduce(
        copy, proj_at, (p_relay_a, p_full_a, p_across_a, p_across_b, p_relay_b, p_full_b), peers
    )
    attention.far()
    attention.middle()
    attention.near()
    running = attention.run()

    def routes(sent):
        first_route, second_route = placed(sent[0:1], sent[1:2])
        weight = first_route * (sent[2:3] + sent[3:4] + sent[4:5])
        weight = weight + second_route * (sent[5:6] + sent[6:7] + sent[7:8])
        return first_route + second_route, weight

    for place in range(8):
        table, weight = routes(xs[place, SEQ:X_ROWS, 0:TOK].astype(F32))
        tables[place] = table.astype(BF)
        high = weight.astype(BF)
        combine[0, place] = high
        combine[1, place] = (weight - high.astype(F32)).astype(BF)

    def combined(high, low, outputs):
        over_slots = (((0,), (0,)), ((), ()))
        total = lax.dot_general(high, outputs, over_slots, preferred_element_type=F32)
        return total + lax.dot_general(low, outputs, over_slots, preferred_element_type=F32)

    for _ in running:
        pass
    state[:, PROJ_CUT:] = (state[:, PROJ_CUT:] + attention.sum_b).astype(BF).astype(F32)
    state[:, :PROJ_CUT] = (state[:, :PROJ_CUT] + attention.sum_a).astype(BF).astype(F32)
    state_now = state[...]
    factor2 = lax.rsqrt(jnp.mean(state_now * state_now, axis=1, keepdims=True) + epsilon)
    ffn_in = (state_now * factor2 * gain2_ref[...].astype(F32)).astype(BF)

    tokens[OWN] = ffn_in[:, SPLIT:]

    spread = Gather(copy, cut_at(lambda place: (tokens.at[place], 0), TOK, TOKENS_CUT, D - SPLIT), peers)
    spread.step(0)

    outgoing[...] = jnp.dot(tables[OWN], ffn_in[:, :SPLIT], preferred_element_type=F32).astype(BF)
    sends = []
    for columns in (pl.ds(SPLIT_CUT, SPLIT - SPLIT_CUT), pl.ds(0, SPLIT_CUT)):
        copies = []
        for dz, dy in hops:
            e_to, _, k_to = exchange(dz, dy)
            copies.append(
                copy(
                    outgoing.at[pl.ds(pl.multiple_of(e_to * CAP, CAP), CAP), columns],
                    rows.at[OWN, pl.ds(pl.multiple_of(dz * HALF_SLOTS + y * CAP, CAP), CAP), columns],
                    (pipe, e_to, k_to),
                )
            )
            copies[-1].start()
        sends.append(copies)
    own_slots = pl.ds(pl.multiple_of(exp * CAP, CAP), CAP)
    own_block = pl.ds(pl.multiple_of(y * CAP, CAP), CAP)
    rows[OWN, own_block, 0:SPLIT] = outgoing[own_slots, :]

    wide_sends = []

    def widen(group):
        for place in (2 * group, 2 * group + 1):
            block = jnp.dot(tables[place], tokens[place], preferred_element_type=F32).astype(BF)
            wide_out[:, place] = block.reshape(8, CAP, D - SPLIT)
        copies = []
        for dz, dy in hops:
            e_to, _, k_to = exchange(dz, dy)
            copies.append(
                copy(
                    wide_out.at[e_to, pl.ds(2 * group, 2)],
                    rows.at[
                        pl.ds(2 * group, 2),
                        pl.ds(pl.multiple_of(dz * HALF_SLOTS + y * CAP, CAP), CAP),
                        pl.ds(SPLIT, D - SPLIT),
                    ],
                    (pipe, e_to, k_to),
                )
            )
            copies[-1].start()
        for place in (2 * group, 2 * group + 1):
            rows[place, own_block, SPLIT:] = wide_out[exp, place]
        wide_sends.append(copies)

    dispatch = Gather(copy, cut_at(lambda place: (rows.at[place], 0), SLOTS, SPLIT_CUT, SPLIT), peers)
    shares = Reduce(
        copy,
        cut_at(lambda place: (part.at[place], 0), SLOTS, BACK_CUT, SPLIT_BACK),
        (d_relay_a, d_full_a, d_across_a, d_across_b, d_relay_b, d_full_b),
        peers,
    )
    narrow = shares.run()

    spread.step(1)
    widen(0)
    spread.step(2)
    for one in sends[0]:
        one.wait_recv()
    dispatch.step("part 1")
    widen(1)
    spread.step(3)
    widen(2)
    for one in sends[1]:
        one.wait_recv()
    dispatch.step("part 0")
    spread.step(4)
    widen(3)
    state_out[...] = state[:, :SPLIT_BACK].astype(BF)
    state_copy = copy(state_out, state_other, other_core)
    state_copy.start()

    wide_backs = []
    for group in range(4):
        copies = []
        for dz, dy in hops:
            e_to, y_to, k_to = exchange(dz, dy)
            copies.append(
                copy(
                    part.at[
                        pl.ds(2 * group, 2),
                        pl.ds(pl.multiple_of(dz * HALF_SLOTS + y_to * CAP, CAP), CAP),
                        pl.ds(SPLIT_BACK, D - SPLIT_BACK),
                    ],
                    wide_back.at[pl.ds(2 * group, 2), own_slots],
                    (pipe, e_to, k_to),
                )
            )
        wide_backs.append(copies)

    for one in loads[11:]:
        one.wait()

    def expert(group, carry):
        for number in range(4):

            @pl.when(group == number)
            def _(number=number):
                if number == 3:
                    shares.middle()
                dispatch.step(number + 1)
                if number == 2:
                    shares.near()
                for one in wide_sends[number]:
                    one.wait_recv()

        places = pl.ds(group * 2, 2)

        block = rows[places].reshape(2 * SLOTS, D)
        gate = jnp.dot(block, wg[...], preferred_element_type=F32)
        upper = jnp.dot(block, wu[...], preferred_element_type=F32)
        act[...] = (gate / (1.0 + jnp.exp(-gate)) * upper).astype(BF)

        def down(n, inner):
            columns = pl.ds(pl.multiple_of(n * 1024, 1024), 1024)
            block = jnp.dot(act[...], wd[:, columns], preferred_element_type=F32).astype(BF)
            part[places, :, columns] = block.reshape(2, SLOTS, 1024)
            return inner

        lax.fori_loop(0, -(-SPLIT_BACK // 1024), down, 0)

        @pl.when(group == 3)
        def _():
            shares.far()

        lax.fori_loop(-(-SPLIT_BACK // 1024), D // 1024, down, 0)
        for number in range(4):

            @pl.when(group == number)
            def _(number=number):
                for one in wide_backs[number]:
                    one.start()
                for place in (2 * number, 2 * number + 1):
                    wide_back[place, own_slots, :] = part[place, own_block, SPLIT_BACK:]

        return carry

    lax.fori_loop(0, 4, expert, 0)

    sums = Reduce(
        copy,
        cut_at(lambda place: (moe.at[place], 0), TOK, MOE_CUT, D - SPLIT_BACK),
        (m_relay_a, m_full_a, m_across_a, m_across_b, m_relay_b, m_full_b),
        peers,
    )
    wide = sums.run()
    backs = []

    def send_back(columns):
        copies = []
        for dz, dy in hops + [(0, 0)]:
            e_to, y_to, k_to = exchange(dz, dy)
            copies.append(
                copy(
                    final.at[pl.ds(pl.multiple_of(dz * HALF_SLOTS + y_to * CAP, CAP), CAP), columns],
                    returned.at[own_slots, columns],
                    (1 - pipe, e_to, k_to),
                )
            )
            copies[-1].start()
        backs.append(copies)

    for _ in range(3):
        next(narrow)
    for group in range(4):
        for one in wide_backs[group]:
            one.wait_recv()
        for place in (2 * group, 2 * group + 1):
            moe[place] = combined(combine[0, place], combine[1, place], wide_back[place]).astype(BF)
    sums.far()
    sums.middle()
    sums.near()
    for _ in range(3):
        next(narrow)
    meta_copy.wait_recv()
    _, weight = routes(meta_other[:, 0:TOK].astype(F32))
    high = weight.astype(BF)
    low = (weight - high.astype(F32)).astype(BF)
    for _ in range(3):
        next(wide)
    next(narrow)
    final[:, :BACK_CUT] = shares.sum_a.astype(BF)
    send_back(pl.ds(0, BACK_CUT))
    for _ in range(3):
        next(wide)
    for _ in narrow:
        pass
    final[:, BACK_CUT:] = shares.sum_b.astype(BF)
    send_back(pl.ds(BACK_CUT, SPLIT_BACK - BACK_CUT))
    for _ in wide:
        pass
    border = SPLIT_BACK + MOE_CUT
    state_wide[:, MOE_CUT:] = (state[:, border:] + sums.sum_b).astype(BF)
    state_wide[:, :MOE_CUT] = (state[:, SPLIT_BACK:border] + sums.sum_a).astype(BF)
    wide_copy = copy(state_wide, out_ref.at[:, pl.ds(SPLIT_BACK, D - SPLIT_BACK)], other_core)
    wide_copy.start()
    state_copy.wait_recv()
    for copies, columns in zip(backs, (slice(0, BACK_CUT), slice(BACK_CUT, SPLIT_BACK))):
        for one in copies:
            one.wait_recv()
        total = state_other[:, columns].astype(F32) + combined(high, low, returned[:, columns])
        out_ref[:, columns] = total.astype(BF)
    for one in (features, attention, spread, dispatch, shares, sums):
        one.finish()
    for one in sum(sends + wide_sends + wide_backs + backs, [meta_copy, state_copy]):
        one.wait_send()
    wide_copy.wait()


def buffers(rows, cut, width):
    rest = width - cut
    return [
        pltpu.VMEM((4, rows // 2, cut), BF),
        pltpu.VMEM((4, rows, cut), BF),
        pltpu.VMEM((rows, cut), BF),
        pltpu.VMEM((4, rows, rest), BF),
        pltpu.VMEM((2, rows // 2, rest), BF),
        pltpu.VMEM((2, rows, rest), BF),
    ]


def on_device(
    inputs,
    attn_gain,
    query_weight,
    key_weight,
    value_weight,
    out_weight,
    ffn_gain,
    gate_weight,
    up_weight,
    down_weight,
    expert_ids,
    route_weights,
):
    cosine, sine = rope_tables()
    anywhere = pl.BlockSpec(memory_space=pl.ANY)
    handed = pl.pallas_call(
        layer,
        out_shape=jax.ShapeDtypeStruct((TOK, D), BF),
        in_specs=[anywhere] * 14,
        out_specs=pl.BlockSpec(memory_space=pltpu.VMEM),
        scratch_shapes=[
            pltpu.VMEM((2, TOK), jnp.int32),
            pltpu.VMEM((2, TOK), F32),
            pltpu.VMEM((1, D), BF),
            pltpu.VMEM((1, D), BF),
            pltpu.VMEM((SEQ, HD), F32),
            pltpu.VMEM((SEQ, HD), F32),
            pltpu.VMEM((D, QKV), BF),
            pltpu.VMEM((384, D), BF),
            pltpu.VMEM((D, HID), BF),
            pltpu.VMEM((D, HID), BF),
            pltpu.VMEM((HID, D), BF),
            pltpu.VMEM((8, X_ROWS, COLS), BF),
            pltpu.VMEM((SEQ, QKV), F32),
            pltpu.VMEM((SEQ, QKV), BF),
            pltpu.VMEM((SEQ, 384), BF),
            pltpu.VMEM((SEQ, D), BF),
            pltpu.VMEM((TOK, D), F32),
            pltpu.VMEM((8, SLOTS, TOK), BF),
            pltpu.VMEM((2, 8, SLOTS, TOK), BF),
            pltpu.VMEM((SLOTS, SPLIT), BF),
            pltpu.VMEM((8, TOK, D - SPLIT), BF),
            pltpu.VMEM((8, 8, CAP, D - SPLIT), BF),
            pltpu.VMEM((8, SLOTS, D), BF),
            pltpu.VMEM((2 * SLOTS, HID), BF),
            pltpu.VMEM((8, SLOTS, D), BF),
            pltpu.VMEM((SLOTS, SPLIT_BACK), BF),
            pltpu.VMEM((SLOTS, SPLIT_BACK), BF),
            pltpu.VMEM((8, SLOTS, D - SPLIT_BACK), BF),
            pltpu.VMEM((8, TOK, D - SPLIT_BACK), BF),
            pltpu.VMEM((TOK, SPLIT_BACK), BF),
            pltpu.VMEM((TOK, SPLIT_BACK), BF),
            pltpu.VMEM((TOK, D - SPLIT_BACK), BF),
            pltpu.VMEM((META, COLS), BF),
            *buffers(TOK, PROJ_CUT, D),
            *buffers(SLOTS, BACK_CUT, SPLIT_BACK),
            *buffers(TOK, MOE_CUT, D - SPLIT_BACK),
            pltpu.SemaphoreType.DMA((14,)),
            pltpu.SemaphoreType.DMA((216,)),
            pltpu.SemaphoreType.DMA((216,)),
        ],
        compiler_params=pltpu.CompilerParams(
            collective_id=0, has_side_effects=True, vmem_limit_bytes=60 * 2**20
        ),
        cost_estimate=pl.CostEstimate(flops=22_000_000_000, bytes_accessed=26_000_000, transcendentals=0),
        name="layer",
    )(
        inputs[0],
        attn_gain,
        query_weight[0],
        key_weight[0],
        value_weight[0],
        out_weight[0],
        ffn_gain,
        gate_weight[0, 0],
        up_weight[0, 0],
        down_weight[0, 0],
        expert_ids[0].T,
        route_weights[0].T,
        jnp.asarray(cosine),
        jnp.asarray(sine),
    )
    return handed[None]


def solution(mesh):
    in_specs = (
        P("pipe", "exp", "etp"),
        P("pipe", None),
        P("pipe", None, "etp"),
        P("pipe", None, "etp"),
        P("pipe", None, "etp"),
        P("pipe", "etp", None),
        P("pipe", None),
        P("pipe", "exp", None, "etp"),
        P("pipe", "exp", None, "etp"),
        P("pipe", "exp", "etp", None),
        P("pipe", ("exp", "etp"), None),
        P("pipe", ("exp", "etp"), None),
    )
    out_specs = P("pipe", ("exp", "etp"), None)
    return jax.shard_map(
        on_device, mesh=mesh, in_specs=in_specs, out_specs=out_specs, check_vma=False
    )
```

```python
import jax
import jax.numpy as jnp
import numpy as np
from jax import lax
from jax.experimental import pallas as pl
from jax.experimental.pallas import tpu as pltpu
from jax.sharding import PartitionSpec as P

D = 3072
HQ = 24
HK = 8
HD = 128
CAP = 16
SEQ = 256
TOK = 32
COLS = D // 8
QKV = 640
HID = 1024

epsilon = 1e-05
rope_base = 1000000.0

MESH = pl.DeviceIdType.MESH
BF = jnp.bfloat16
F32 = jnp.float32

OWN, Z, L, R, LZ, RZ, O, OZ = range(8)
SLOTS = 8 * CAP
HALF_SLOTS = SLOTS // 2
SPLIT = 2048
SPLIT_BACK = 2048
PROJ_CUT = 1664
TOKENS_CUT = 640
SPLIT_CUT = 1152
BACK_CUT = 1024
MOE_CUT = 640
META = 16
X_ROWS = SEQ + META


def rope_tables():
    half = HD // 2
    angles = np.arange(SEQ)[:, None] * rope_base ** (-np.arange(half) / half)[None, :]
    cosine, sine = np.cos(angles), np.sin(angles)
    return (
        np.concatenate([cosine, cosine], axis=1).astype(np.float32),
        np.concatenate([-sine, sine], axis=1).astype(np.float32),
    )


class Gather:
    def __init__(self, copy, at, peers):
        left, right, across = peers

        def plan(place, part, half, device, there):
            return lambda: copy(at(place, part, half), at(there, part, half), device)

        steps = {
            "a_z": plan(OWN, 0, None, across, Z),
            "a_l": plan(OWN, 0, None, left, R),
            "a_r": plan(OWN, 0, None, right, L),
            "b_z": plan(OWN, 1, None, across, Z),
            "b_l": plan(OWN, 1, None, left, R),
            "b_r": plan(OWN, 1, None, right, L),
            "za_l": plan(Z, 0, None, left, RZ),
            "za_r": plan(Z, 0, None, right, LZ),
            "lb_r": plan(L, 1, 0, right, O),
            "rb_l": plan(R, 1, 1, left, O),
            "lb_z": plan(L, 1, None, across, LZ),
            "rb_z": plan(R, 1, None, across, RZ),
            "la_r": plan(L, 0, 0, right, O),
            "ra_l": plan(R, 0, 1, left, O),
            "lza_r": plan(LZ, 0, 0, right, OZ),
            "rza_l": plan(RZ, 0, 1, left, OZ),
            "ob_z": plan(O, 1, None, across, OZ),
        }
        self.copies = {name: make() for name, make in steps.items()}

    def start(self, *names):
        for name in names:
            self.copies[name].start()

    def arrive(self, *names):
        for name in names:
            self.copies[name].wait_recv()

    def step(self, number):
        if number == 0:
            self.start("b_r", "b_l", "a_z", "a_r", "a_l", "b_z")
        if number == "part 0":
            self.start("a_z", "a_r", "a_l")
        if number == "part 1":
            self.start("b_r", "b_l", "b_z")
        if number == 1:
            self.arrive("b_r")
            self.start("lb_r", "lb_z")
            self.arrive("b_l")
            self.start("rb_l", "rb_z")
            self.arrive("a_z")
            self.start("za_r", "za_l")
            self.arrive("b_z")
        if number == 2:
            self.arrive("a_r", "a_l")
            self.start("la_r", "ra_l")
            self.arrive("lb_r", "rb_l")
            self.start("ob_z")
        if number == 3:
            self.arrive("za_r", "za_l")
            self.start("lza_r", "rza_l")
            self.arrive("lb_z", "rb_z")
        if number == 4:
            self.arrive("la_r", "ra_l", "lza_r", "rza_l", "ob_z")

    def finish(self):
        for one in self.copies.values():
            one.wait_send()


class Reduce:
    def __init__(self, copy, at, buffers, peers):
        left, right, across = peers
        self.at = at
        self.relay_a, self.full_a, self.across_a, self.across_b, self.relay_b, self.full_b = buffers

        def halved(ref, i, half):
            count = ref.shape[1] // 2
            return ref.at[i, pl.ds(half * count, count)]

        self.copies = {
            "oz_r": copy(at(OZ, 0, 0), self.relay_a.at[2], right),
            "oz_l": copy(at(OZ, 0, 1), self.relay_a.at[3], left),
            "o_r": copy(at(O, 0, 0), self.relay_a.at[0], right),
            "o_l": copy(at(O, 0, 1), self.relay_a.at[1], left),
            "z_z": copy(at(Z, 0, None), self.across_a, across),
            "b_own": copy(at(Z, 1, None), self.across_b.at[0], across),
            "b_left": copy(at(LZ, 1, None), self.across_b.at[1], across),
            "b_right": copy(at(RZ, 1, None), self.across_b.at[2], across),
            "b_opp": copy(at(OZ, 1, None), self.across_b.at[3], across),
            "bo_r": copy(at(O, 1, 0), self.relay_b.at[0], right),
            "bo_l": copy(at(O, 1, 1), self.relay_b.at[1], left),
        }
        for half in (0, 1):
            self.copies["rz%d" % half] = copy(at(RZ, 0, half), halved(self.full_a, 2, half), right)
            self.copies["lz%d" % half] = copy(at(LZ, 0, half), halved(self.full_a, 3, half), left)
            self.copies["r%d" % half] = copy(at(R, 0, half), halved(self.full_a, 0, half), right)
            self.copies["l%d" % half] = copy(at(L, 0, half), halved(self.full_a, 1, half), left)
            self.copies["br%d" % half] = copy(at(R, 1, half), halved(self.full_b, 0, half), right)
            self.copies["bl%d" % half] = copy(at(L, 1, half), halved(self.full_b, 1, half), left)

    def start(self, *names):
        for name in names:
            self.copies[name].start()

    def arrive(self, *names):
        for name in names:
            self.copies[name].wait_recv()

    def add(self, place, part, half, *terms):
        ref = self.at(place, part, half)
        total = ref[...].astype(F32)
        for term in terms:
            total = total + term[...].astype(F32)
        ref[...] = total.astype(BF)

    def total(self, part, *terms):
        result = self.at(OWN, part, None)[...].astype(F32)
        for term in terms:
            result = result + term.astype(F32)
        return result

    def near(self):
        self.start("r1", "l0", "b_own")

    def middle(self):
        self.start("rz1", "lz0", "b_left")

    def far_along_x(self):
        self.start("oz_r", "oz_l", "o_r", "o_l")

    def far_along_z(self):
        self.start("b_opp", "b_right")

    def far(self):
        self.far_along_z()
        self.far_along_x()

    def run(self):
        self.arrive("oz_r")
        self.add(RZ, 0, 0, self.relay_a.at[2])
        self.start("rz0")
        self.arrive("oz_l")
        self.add(LZ, 0, 1, self.relay_a.at[3])
        self.start("lz1")
        yield
        self.arrive("b_opp")
        self.add(O, 1, None, self.across_b.at[3])
        self.start("bo_r", "bo_l")
        yield
        self.arrive("o_r")
        self.add(R, 0, 0, self.relay_a.at[0])
        self.start("r0")
        self.arrive("o_l")
        self.add(L, 0, 1, self.relay_a.at[1])
        self.start("l1")
        yield
        self.arrive("rz0", "rz1", "lz0", "lz1")
        self.add(Z, 0, None, self.full_a.at[2], self.full_a.at[3])
        self.start("z_z")
        yield
        self.arrive("b_right")
        self.add(R, 1, None, self.across_b.at[2])
        self.start("br1")
        self.arrive("b_left")
        self.add(L, 1, None, self.across_b.at[1])
        self.start("bl0")
        yield
        self.arrive("bo_r")
        self.add(R, 1, 0, self.relay_b.at[0])
        self.start("br0")
        self.arrive("bo_l")
        self.add(L, 1, 1, self.relay_b.at[1])
        self.start("bl1")
        yield
        self.arrive("r0", "r1", "l0", "l1", "z_z")
        self.sum_a = self.total(0, self.full_a[0], self.full_a[1], self.across_a[...])
        yield
        self.arrive("b_own", "br0", "br1", "bl0", "bl1")
        self.sum_b = self.total(1, self.across_b[0], self.full_b[0], self.full_b[1])

    def finish(self):
        for one in self.copies.values():
            one.wait_send()


def placed(first_ids, second_ids):
    slot_row = lax.broadcasted_iota(jnp.int32, (SLOTS, TOK), 0)
    expert = (slot_row // CAP).astype(F32)
    first_route = (first_ids == expert).astype(F32)
    second_route = (second_ids == expert).astype(F32)
    earlier = (
        lax.broadcasted_iota(jnp.int32, (TOK, TOK), 0) < lax.broadcasted_iota(jnp.int32, (TOK, TOK), 1)
    ).astype(BF)
    before = jnp.dot((first_route + second_route).astype(BF), earlier, preferred_element_type=F32)
    here = (before == (slot_row % CAP).astype(F32)).astype(F32)
    return first_route * here, second_route * here


def split_in_three(values):
    high = values.astype(BF).astype(F32)
    middle = (values - high).astype(BF).astype(F32)
    return high, middle, values - high - middle


def layer(
    x_ref, gain1_hbm, wq_ref, wk_ref, wv_ref, wo_ref, gain2_hbm, wg_ref, wu_ref, wd_ref, ids_hbm, weights_hbm,
    cos_hbm, sin_hbm, out_ref,
    ids_ref, weights_ref, gain1_ref, gain2_ref, cos_ref, sin_ref,
    wqkv, wo, wg, wu, wd, xs, acc, heads, mixed, proj, state, tables, combine, outgoing, tokens, wide_out, rows, act,
    part, final, returned, wide_back, moe, state_out, state_other, state_wide, meta_other,
    p_relay_a, p_full_a, p_across_a, p_across_b, p_relay_b, p_full_b,
    d_relay_a, d_full_a, d_across_a, d_across_b, d_relay_b, d_full_b,
    m_relay_a, m_full_a, m_across_a, m_across_b, m_relay_b, m_full_b,
    load_sem, send_sem, recv_sem,
):
    pipe, exp, etp = lax.axis_index("pipe"), lax.axis_index("exp"), lax.axis_index("etp")
    zh, y = exp // 4, exp % 4
    zl, x = etp // 4, etp % 4

    def ring(zl_to, step):
        return zl_to * 4 + (x + step) % 4

    index_of = {
        OWN: etp, Z: ring(1 - zl, 0), L: ring(zl, 3), R: ring(zl, 1),
        LZ: ring(1 - zl, 3), RZ: ring(1 - zl, 1), O: ring(zl, 2), OZ: ring(1 - zl, 2),
    }
    peers = tuple((pipe, exp, index_of[place]) for place in (L, R, Z))

    def exchange(dz, dy):
        zh_to, y_to = (zh + dz) % 2, (y + dy) % 4
        return zh_to * 4 + y_to, y_to, (etp if dz == 0 else index_of[Z])

    hops = [(dz, dy) for dy in (2, 1, 3, 0) for dz in (1, 0) if (dz, dy) != (0, 0)]
    other_core = (1 - pipe, exp, etp)

    barrier = pltpu.get_barrier_semaphore()
    for device in peers:
        pl.semaphore_signal(barrier, inc=1, device_id=device, device_id_type=MESH)
    for dz, dy in hops:
        e_to, _, k_to = exchange(dz, dy)
        for section in (pipe, 1 - pipe):
            pl.semaphore_signal(barrier, inc=1, device_id=(section, e_to, k_to), device_id_type=MESH)
    pl.semaphore_signal(barrier, inc=1, device_id=other_core, device_id_type=MESH)

    loads = [
        pltpu.make_async_copy(source, target, load_sem.at[i])
        for i, (source, target) in enumerate(
            (
                (ids_hbm, ids_ref),
                (weights_hbm, weights_ref),
                (x_ref, xs.at[0, pl.ds(0, SEQ)]),
                (gain1_hbm, gain1_ref),
                (wq_ref, wqkv.at[:, pl.ds(0, 384)]),
                (wk_ref, wqkv.at[:, pl.ds(384, 128)]),
                (wv_ref, wqkv.at[:, pl.ds(512, 128)]),
                (cos_hbm, cos_ref),
                (sin_hbm, sin_ref),
                (wo_ref, wo),
                (gain2_hbm, gain2_ref),
                (wg_ref, wg),
                (wu_ref, wu),
                (wd_ref, wd),
            )
        )
    ]
    for one in loads:
        one.start()

    for one in loads[:2]:
        one.wait()
    xs[0, SEQ:X_ROWS, :] = jnp.zeros((META, COLS), BF)
    meta_row = lax.broadcasted_iota(jnp.int32, (META, TOK), 0)
    meta_rows = [ids_ref[0:1, :].astype(F32), ids_ref[1:2, :].astype(F32)]
    meta_rows += [*split_in_three(weights_ref[0:1, :]), *split_in_three(weights_ref[1:2, :])]
    meta = jnp.zeros((META, TOK), F32)
    for i, row in enumerate(meta_rows):
        meta = jnp.where(meta_row == i, row, meta)
    xs[0, SEQ:X_ROWS, 0:TOK] = meta.astype(BF)
    loads[2].wait()
    pl.semaphore_wait(barrier, 4 + 2 * len(hops))

    used = [0]

    def copy(source, target, device):
        i = used[0]
        used[0] = i + 1
        return pltpu.make_async_remote_copy(
            src_ref=source, dst_ref=target, send_sem=send_sem.at[i], recv_sem=recv_sem.at[i],
            device_id=device, device_id_type=MESH,
        )

    x_parts = {
        (0, None): (0, 144), (0, 0): (0, 80), (0, 1): (80, 64),
        (1, None): (144, 128), (1, 0): (144, 64), (1, 1): (208, 64),
    }

    def xs_at(place, part_no, half):
        return xs.at[place, pl.ds(*x_parts[part_no, half])]

    features = Gather(copy, xs_at, peers)
    squares = []

    def project(place):
        offset = pl.multiple_of(index_of[place] * COLS, 128)
        block = xs[place, 0:SEQ, :].astype(F32)
        squares.append(jnp.sum(block * block, axis=1, keepdims=True))
        scaled = (block * gain1_ref[:, pl.ds(offset, COLS)].astype(F32)).astype(BF)
        term = jnp.dot(scaled, wqkv[pl.ds(offset, COLS), :], preferred_element_type=F32)
        acc[...] = term if place == OWN else acc[...] + term
        own_rows = pl.ds(pl.multiple_of(etp * TOK, TOK), TOK)
        state[:, pl.ds(offset, COLS)] = xs[place, own_rows, :].astype(F32)

    features.step(0)
    meta_copy = copy(xs.at[OWN, pl.ds(SEQ, META)], meta_other, other_core)
    meta_copy.start()
    for one in loads[3:7]:
        one.wait()
    project(OWN)
    features.step(1)
    features.step(2)
    for place in (Z, L, R):
        project(place)
    features.step(3)
    for place in (LZ, RZ):
        project(place)
    features.step(4)
    for place in (O, OZ):
        project(place)

    for one in loads[7:11]:
        one.wait()
    factor = lax.rsqrt(sum(squares) * (1.0 / D) + epsilon)
    for i in range(5):
        block = acc[:, i * HD : (i + 1) * HD] * factor
        if i < 4:
            block = block * cos_ref[...] + pltpu.roll(block, HD // 2, 1) * sin_ref[...]
        heads[:, i * HD : (i + 1) * HD] = block.astype(BF)
    causal = lax.broadcasted_iota(jnp.int32, (SEQ, SEQ), 0) >= lax.broadcasted_iota(jnp.int32, (SEQ, SEQ), 1)
    keys, values = heads[:, 384:512], heads[:, 512:640]
    for i in range(3):
        scores = lax.dot_general(
            heads[:, i * HD : (i + 1) * HD], keys, (((1,), (1,)), ((), ())), preferred_element_type=F32
        ) * HD ** (-0.5)
        scores = jnp.where(causal, scores, -1e30)
        expo = jnp.exp(scores - jnp.max(scores, axis=1, keepdims=True))
        probs = (expo / jnp.sum(expo, axis=1, keepdims=True)).astype(BF)
        mixed[:, i * HD : (i + 1) * HD] = jnp.dot(probs, values, preferred_element_type=F32).astype(BF)

    def out_columns(n, carry):
        columns = pl.ds(pl.multiple_of(n * 512, 512), 512)
        proj[:, columns] = jnp.dot(mixed[...], wo[:, columns], preferred_element_type=F32).astype(BF)
        return carry

    def cut_at(block_of, count, cut, width):
        def at(place, part_no, half):
            ref, first = block_of(place)
            rows_here = pl.ds(first, count)
            if half is not None:
                rows_here = pl.ds(first + half * (count // 2), count // 2)
            return ref.at[rows_here, pl.ds(0, cut) if part_no == 0 else pl.ds(cut, width - cut)]

        return at

    def proj_block(place):
        return proj, pl.multiple_of(index_of[place] * TOK, TOK)

    proj_at = cut_at(proj_block, TOK, PROJ_CUT, D)

    attention = Reduce(
        copy, proj_at, (p_relay_a, p_full_a, p_across_a, p_across_b, p_relay_b, p_full_b), peers
    )
    lax.fori_loop(0, -(-PROJ_CUT // 512), out_columns, 0)
    attention.far_along_x()
    lax.fori_loop(-(-PROJ_CUT // 512), D // 512, out_columns, 0)
    attention.far_along_z()
    attention.middle()
    attention.near()
    running = attention.run()

    def routes(sent):
        first_route, second_route = placed(sent[0:1], sent[1:2])
        weight = first_route * (sent[2:3] + sent[3:4] + sent[4:5])
        weight = weight + second_route * (sent[5:6] + sent[6:7] + sent[7:8])
        return first_route + second_route, weight

    def place_tokens(first, last):
        for place in range(first, last):
            table, _ = routes(xs[place, SEQ:X_ROWS, 0:TOK].astype(F32))
            tables[place] = table.astype(BF)

    place_tokens(0, 2)

    def combined(high, low, outputs):
        over_slots = (((0,), (0,)), ((), ()))
        total = lax.dot_general(high, outputs, over_slots, preferred_element_type=F32)
        return total + lax.dot_general(low, outputs, over_slots, preferred_element_type=F32)

    next(running)
    place_tokens(2, 4)
    next(running)
    next(running)
    place_tokens(4, 8)
    for _ in running:
        pass
    state[:, PROJ_CUT:] = (state[:, PROJ_CUT:] + attention.sum_b).astype(BF).astype(F32)
    state[:, :PROJ_CUT] = (state[:, :PROJ_CUT] + attention.sum_a).astype(BF).astype(F32)
    state_now = state[...]
    factor2 = lax.rsqrt(jnp.mean(state_now * state_now, axis=1, keepdims=True) + epsilon)
    ffn_in = (state_now * factor2 * gain2_ref[...].astype(F32)).astype(BF)

    tokens[OWN] = ffn_in[:, SPLIT:]

    spread = Gather(copy, cut_at(lambda place: (tokens.at[place], 0), TOK, TOKENS_CUT, D - SPLIT), peers)
    spread.step(0)

    outgoing[...] = jnp.dot(tables[OWN], ffn_in[:, :SPLIT], preferred_element_type=F32).astype(BF)
    sends = []
    for columns in (pl.ds(SPLIT_CUT, SPLIT - SPLIT_CUT), pl.ds(0, SPLIT_CUT)):
        copies = []
        for dz, dy in hops:
            e_to, _, k_to = exchange(dz, dy)
            copies.append(
                copy(
                    outgoing.at[pl.ds(pl.multiple_of(e_to * CAP, CAP), CAP), columns],
                    rows.at[OWN, pl.ds(pl.multiple_of(dz * HALF_SLOTS + y * CAP, CAP), CAP), columns],
                    (pipe, e_to, k_to),
                )
            )
            copies[-1].start()
        sends.append(copies)
    own_slots = pl.ds(pl.multiple_of(exp * CAP, CAP), CAP)
    own_block = pl.ds(pl.multiple_of(y * CAP, CAP), CAP)
    rows[OWN, own_block, 0:SPLIT] = outgoing[own_slots, :]

    wide_sends = []

    def widen(group):
        for place in (2 * group, 2 * group + 1):
            block = jnp.dot(tables[place], tokens[place], preferred_element_type=F32).astype(BF)
            wide_out[:, place] = block.reshape(8, CAP, D - SPLIT)
        copies = []
        for dz, dy in hops:
            e_to, _, k_to = exchange(dz, dy)
            copies.append(
                copy(
                    wide_out.at[e_to, pl.ds(2 * group, 2)],
                    rows.at[
                        pl.ds(2 * group, 2),
                        pl.ds(pl.multiple_of(dz * HALF_SLOTS + y * CAP, CAP), CAP),
                        pl.ds(SPLIT, D - SPLIT),
                    ],
                    (pipe, e_to, k_to),
                )
            )
            copies[-1].start()
        for place in (2 * group, 2 * group + 1):
            rows[place, own_block, SPLIT:] = wide_out[exp, place]
        wide_sends.append(copies)

    dispatch = Gather(copy, cut_at(lambda place: (rows.at[place], 0), SLOTS, SPLIT_CUT, SPLIT), peers)
    shares = Reduce(
        copy,
        cut_at(lambda place: (part.at[place], 0), SLOTS, BACK_CUT, SPLIT_BACK),
        (d_relay_a, d_full_a, d_across_a, d_across_b, d_relay_b, d_full_b),
        peers,
    )
    narrow = shares.run()

    spread.step(1)
    widen(0)
    spread.step(2)
    for one in sends[0]:
        one.wait_recv()
    dispatch.step("part 1")
    widen(1)
    spread.step(3)
    widen(2)
    for one in sends[1]:
        one.wait_recv()
    dispatch.step("part 0")
    spread.step(4)
    widen(3)
    state_out[...] = state[:, :SPLIT_BACK].astype(BF)
    state_copy = copy(state_out, state_other, other_core)
    state_copy.start()

    wide_backs = []
    for group in range(4):
        copies = []
        for dz, dy in hops:
            e_to, y_to, k_to = exchange(dz, dy)
            copies.append(
                copy(
                    part.at[
                        pl.ds(2 * group, 2),
                        pl.ds(pl.multiple_of(dz * HALF_SLOTS + y_to * CAP, CAP), CAP),
                        pl.ds(SPLIT_BACK, D - SPLIT_BACK),
                    ],
                    wide_back.at[pl.ds(2 * group, 2), own_slots],
                    (pipe, e_to, k_to),
                )
            )
        wide_backs.append(copies)

    for place in range(8):
        _, weight = routes(xs[place, SEQ:X_ROWS, 0:TOK].astype(F32))
        high = weight.astype(BF)
        combine[0, place] = high
        combine[1, place] = (weight - high.astype(F32)).astype(BF)
    for one in loads[11:]:
        one.wait()
    for one in (features, attention):
        one.finish()
    meta_copy.wait_send()

    def expert(group, carry):
        for number in range(4):

            @pl.when(group == number)
            def _(number=number):
                if number == 3:
                    shares.middle()
                dispatch.step(number + 1)
                if number == 2:
                    shares.near()
                for one in wide_sends[number]:
                    one.wait_recv()

        places = pl.ds(group * 2, 2)

        block = rows[places].reshape(2 * SLOTS, D)
        gate = jnp.dot(block, wg[...], preferred_element_type=F32)
        upper = jnp.dot(block, wu[...], preferred_element_type=F32)
        act[...] = (gate / (1.0 + jnp.exp(-gate)) * upper).astype(BF)

        def down(n, inner):
            columns = pl.ds(pl.multiple_of(n * 1024, 1024), 1024)
            block = jnp.dot(act[...], wd[:, columns], preferred_element_type=F32).astype(BF)
            part[places, :, columns] = block.reshape(2, SLOTS, 1024)
            return inner

        steps = (0, -(-BACK_CUT // 1024), -(-SPLIT_BACK // 1024), D // 1024)
        lax.fori_loop(steps[0], steps[1], down, 0)

        @pl.when(group == 3)
        def _():
            shares.far_along_x()

        lax.fori_loop(steps[1], steps[2], down, 0)

        @pl.when(group == 3)
        def _():
            shares.far_along_z()

        lax.fori_loop(steps[2], steps[3], down, 0)
        for number in range(4):

            @pl.when(group == number)
            def _(number=number):
                for one in wide_backs[number]:
                    one.start()
                for place in (2 * number, 2 * number + 1):
                    wide_back[place, own_slots, :] = part[place, own_block, SPLIT_BACK:]

        return carry

    lax.fori_loop(0, 4, expert, 0)

    sums = Reduce(
        copy,
        cut_at(lambda place: (moe.at[place], 0), TOK, MOE_CUT, D - SPLIT_BACK),
        (m_relay_a, m_full_a, m_across_a, m_across_b, m_relay_b, m_full_b),
        peers,
    )
    wide = sums.run()
    backs = []

    def send_back(columns):
        copies = []
        for dz, dy in hops + [(0, 0)]:
            e_to, y_to, k_to = exchange(dz, dy)
            copies.append(
                copy(
                    final.at[pl.ds(pl.multiple_of(dz * HALF_SLOTS + y_to * CAP, CAP), CAP), columns],
                    returned.at[own_slots, columns],
                    (1 - pipe, e_to, k_to),
                )
            )
            copies[-1].start()
        backs.append(copies)

    for _ in range(3):
        next(narrow)
    for group in range(4):
        for one in wide_backs[group]:
            one.wait_recv()
        for place in (2 * group, 2 * group + 1):
            moe[place] = combined(combine[0, place], combine[1, place], wide_back[place]).astype(BF)
    sums.far()
    sums.middle()
    sums.near()
    for _ in range(3):
        next(narrow)
    meta_copy.wait_recv()
    _, weight = routes(meta_other[:, 0:TOK].astype(F32))
    high = weight.astype(BF)
    low = (weight - high.astype(F32)).astype(BF)
    for one in (spread, dispatch):
        one.finish()
    for one in sum(sends + wide_sends, [state_copy]):
        one.wait_send()
    for _ in range(3):
        next(wide)
    next(narrow)
    final[:, :BACK_CUT] = shares.sum_a.astype(BF)
    send_back(pl.ds(0, BACK_CUT))
    for _ in range(3):
        next(wide)
    for _ in narrow:
        pass
    final[:, BACK_CUT:] = shares.sum_b.astype(BF)
    send_back(pl.ds(BACK_CUT, SPLIT_BACK - BACK_CUT))
    shares.finish()
    for one in sum(wide_backs, []):
        one.wait_send()
    for _ in wide:
        pass
    border = SPLIT_BACK + MOE_CUT
    state_wide[:, MOE_CUT:] = (state[:, border:] + sums.sum_b).astype(BF)
    state_wide[:, :MOE_CUT] = (state[:, SPLIT_BACK:border] + sums.sum_a).astype(BF)
    wide_copy = copy(state_wide, out_ref.at[:, pl.ds(SPLIT_BACK, D - SPLIT_BACK)], other_core)
    wide_copy.start()
    sums.finish()
    state_copy.wait_recv()
    for copies, columns in zip(backs, (slice(0, BACK_CUT), slice(BACK_CUT, SPLIT_BACK))):
        for one in copies:
            one.wait_recv()
        total = state_other[:, columns].astype(F32) + combined(high, low, returned[:, columns])
        out_ref[:, columns] = total.astype(BF)
    for one in sum(backs, []):
        one.wait_send()
    wide_copy.wait()


def buffers(rows, cut, width):
    rest = width - cut
    return [
        pltpu.VMEM((4, rows // 2, cut), BF),
        pltpu.VMEM((4, rows, cut), BF),
        pltpu.VMEM((rows, cut), BF),
        pltpu.VMEM((4, rows, rest), BF),
        pltpu.VMEM((2, rows // 2, rest), BF),
        pltpu.VMEM((2, rows, rest), BF),
    ]


def on_device(
    inputs,
    attn_gain,
    query_weight,
    key_weight,
    value_weight,
    out_weight,
    ffn_gain,
    gate_weight,
    up_weight,
    down_weight,
    expert_ids,
    route_weights,
):
    cosine, sine = rope_tables()
    anywhere = pl.BlockSpec(memory_space=pl.ANY)
    handed = pl.pallas_call(
        layer,
        out_shape=jax.ShapeDtypeStruct((TOK, D), BF),
        in_specs=[anywhere] * 14,
        out_specs=pl.BlockSpec(memory_space=pltpu.VMEM),
        scratch_shapes=[
            pltpu.VMEM((2, TOK), jnp.int32),
            pltpu.VMEM((2, TOK), F32),
            pltpu.VMEM((1, D), BF),
            pltpu.VMEM((1, D), BF),
            pltpu.VMEM((SEQ, HD), F32),
            pltpu.VMEM((SEQ, HD), F32),
            pltpu.VMEM((D, QKV), BF),
            pltpu.VMEM((384, D), BF),
            pltpu.VMEM((D, HID), BF),
            pltpu.VMEM((D, HID), BF),
            pltpu.VMEM((HID, D), BF),
            pltpu.VMEM((8, X_ROWS, COLS), BF),
            pltpu.VMEM((SEQ, QKV), F32),
            pltpu.VMEM((SEQ, QKV), BF),
            pltpu.VMEM((SEQ, 384), BF),
            pltpu.VMEM((SEQ, D), BF),
            pltpu.VMEM((TOK, D), F32),
            pltpu.VMEM((8, SLOTS, TOK), BF),
            pltpu.VMEM((2, 8, SLOTS, TOK), BF),
            pltpu.VMEM((SLOTS, SPLIT), BF),
            pltpu.VMEM((8, TOK, D - SPLIT), BF),
            pltpu.VMEM((8, 8, CAP, D - SPLIT), BF),
            pltpu.VMEM((8, SLOTS, D), BF),
            pltpu.VMEM((2 * SLOTS, HID), BF),
            pltpu.VMEM((8, SLOTS, D), BF),
            pltpu.VMEM((SLOTS, SPLIT_BACK), BF),
            pltpu.VMEM((SLOTS, SPLIT_BACK), BF),
            pltpu.VMEM((8, SLOTS, D - SPLIT_BACK), BF),
            pltpu.VMEM((8, TOK, D - SPLIT_BACK), BF),
            pltpu.VMEM((TOK, SPLIT_BACK), BF),
            pltpu.VMEM((TOK, SPLIT_BACK), BF),
            pltpu.VMEM((TOK, D - SPLIT_BACK), BF),
            pltpu.VMEM((META, COLS), BF),
            *buffers(TOK, PROJ_CUT, D),
            *buffers(SLOTS, BACK_CUT, SPLIT_BACK),
            *buffers(TOK, MOE_CUT, D - SPLIT_BACK),
            pltpu.SemaphoreType.DMA((14,)),
            pltpu.SemaphoreType.DMA((216,)),
            pltpu.SemaphoreType.DMA((216,)),
        ],
        compiler_params=pltpu.CompilerParams(
            collective_id=0, has_side_effects=True, vmem_limit_bytes=60 * 2**20
        ),
        cost_estimate=pl.CostEstimate(flops=22_000_000_000, bytes_accessed=26_000_000, transcendentals=0),
        name="layer",
    )(
        inputs[0],
        attn_gain,
        query_weight[0],
        key_weight[0],
        value_weight[0],
        out_weight[0],
        ffn_gain,
        gate_weight[0, 0],
        up_weight[0, 0],
        down_weight[0, 0],
        expert_ids[0].T,
        route_weights[0].T,
        jnp.asarray(cosine),
        jnp.asarray(sine),
    )
    return handed[None]


def solution(mesh):
    in_specs = (
        P("pipe", "exp", "etp"),
        P("pipe", None),
        P("pipe", None, "etp"),
        P("pipe", None, "etp"),
        P("pipe", None, "etp"),
        P("pipe", "etp", None),
        P("pipe", None),
        P("pipe", "exp", None, "etp"),
        P("pipe", "exp", None, "etp"),
        P("pipe", "exp", "etp", None),
        P("pipe", ("exp", "etp"), None),
        P("pipe", ("exp", "etp"), None),
    )
    out_specs = P("pipe", ("exp", "etp"), None)
    return jax.shard_map(
        on_device, mesh=mesh, in_specs=in_specs, out_specs=out_specs, check_vma=False
    )
```
